128 devices in a mesh: dp: 16 (over y, x_lo, core), tensor: 8 (over z, x_hi).
Axes of the slice: x: 4 (x_hi: 2, x_lo: 2; x = x_hi * 2 + x_lo), y: 4, z: 4, core: 2. Of those that a mesh axis runs over, the one named last changes fastest.
Arguments:
- gate_pre: bfloat16 [8192, 14336], P('dp', 'tensor'), may hold values from -6 to 6
- up_pre: bfloat16 [8192, 14336], P('dp', 'tensor'), may hold values from -6 to 6
- out_grad: bfloat16 [8192, 4096], P(('dp', 'tensor')), may hold values from -24 to 24
- down_weight: bfloat16 [4096, 14336], P(('dp', 'tensor')), may hold values from -0.046875 to 0.046875
Outputs:
- gate_grad: bfloat16 [8192, 14336], P('dp', 'tensor')
- up_grad: bfloat16 [8192, 14336], P('dp', 'tensor')
- down_grad: bfloat16 [4096, 14336], P('dp', 'tensor')
The draws below stay inside these ranges and needn't reach their ends.
All inputs are finite; a program needn't handle non-finite values.
Results may differ from the reference program's by a relative error of at most 0.022.
Values may be sent and summed in bfloat16 or wider, within the bound.
No kernel may reach another device: no remote copies, remote signals or barrier semaphores. Data moves between devices by JAX's collectives and lax.ppermute only.
A program may use at most 128 MiB of HBM per device.

```python
import jax
import jax.numpy as jnp
from jax import lax

D = 4096
FF = 14336
TOK_DEV = 64
TOKENS = 8192
N_DP = 16
N_TENSOR = 8


def strengthened(array, stream_key, source, target, shards_of, factor):
    owner, partner = [(jnp.arange(array.shape[position]) // (array.shape[position] // shards_of)).reshape([-1 if axis == position else 1 for axis in range(array.ndim)]) for position in (source, target)]
    chosen = jax.random.permutation(stream_key, shards_of)[partner]
    strong = (owner == chosen) | (owner == (partner + shards_of // 2) % shards_of)
    return jnp.where(strong, factor * array, array)


def steps_of(stream_key, shape, pieces, smallest, high):
    def one(axis_at, blocks):
        steps = jax.random.uniform(jax.random.fold_in(jax.random.fold_in(stream_key, 6), axis_at), (blocks,), jnp.float32, smallest / len(pieces), high / len(pieces))
        return jnp.repeat(jnp.exp(steps), shape[axis_at] // blocks).reshape((-1,) + (1,) * (len(shape) - axis_at - 1))

    factor_of = one(*pieces[0])
    for cut in pieces[1:]:
        factor_of = factor_of * one(*cut)
    return factor_of


def normal_values(stream_key, extent, spread, reach, cuts=(), kind=jnp.bfloat16):
    values = jax.random.normal(stream_key, extent, jnp.float32) * spread
    if len(cuts) > 0:
        values = steps_of(stream_key, extent, cuts, -0.22, 0.18) * values
    return jnp.clip(values, min=-reach, max=reach).astype(kind)


def noise_with(own_key, shape, scale, reach, split, heavy, dtype=jnp.bfloat16):
    result = scale * jax.random.normal(own_key, shape, jnp.float32)
    if split:
        result = result * steps_of(own_key, shape, split, -0.22, 0.18)
    return jnp.clip(strengthened(result, jax.random.fold_in(own_key, 3), *heavy), -reach, reach).astype(dtype)


def setup_inputs(seed: int = 0) -> dict:
    arg_keys = jax.random.split(jax.random.key(seed), 5)
    return {
        "gate_pre": normal_values(arg_keys[0], (TOKENS, FF), 1.0, 6.0, ((0, 16), (1, 8))),
        "up_pre": normal_values(arg_keys[1], (TOKENS, FF), 1.0, 6.0, ((0, 16), (1, 8))),
        "out_grad": noise_with(arg_keys[2], (TOKENS, D), 1.0, 24.0, ((0, 128),), (0, 1, 128, 5.5)),
        "down_weight": normal_values(arg_keys[3], (D, FF), FF ** -0.5, 0.046875, ((0, 128),)),
    }


def reference(gate_pre, up_pre, out_grad, down_weight):
    gate_all = gate_pre.reshape(N_DP, TOK_DEV * N_TENSOR, FF)
    up_all = up_pre.reshape(N_DP, TOK_DEV * N_TENSOR, FF)
    grad_all = out_grad.reshape(N_DP, TOK_DEV * N_TENSOR, D)
    factor = 1.0 / jnp.sqrt(jnp.float32(TOK_DEV * N_TENSOR * N_DP))

    def one_group(total, inputs):
        gate_rows, up_rows, grad_rows = inputs
        gate = gate_rows.astype(jnp.float32)
        up = up_rows.astype(jnp.float32)
        sig = jax.nn.sigmoid(gate)
        hidden = (gate * sig * up).astype(jnp.bfloat16)
        hidden_grad = jnp.dot(grad_rows, down_weight, preferred_element_type=jnp.float32)
        gate_out = (hidden_grad * up * sig * (1.0 + gate * (1.0 - sig))).astype(jnp.bfloat16)
        up_out = (hidden_grad * gate * sig).astype(jnp.bfloat16)
        term = (jnp.dot(grad_rows.T, hidden, preferred_element_type=jnp.float32) * factor).astype(jnp.bfloat16)
        return (total + term.astype(jnp.float32), (gate_out, up_out))
    total, (gate_out, up_out) = lax.scan(one_group, jnp.zeros((D, FF), jnp.float32), (gate_all, up_all, grad_all))
    tokens = TOK_DEV * N_TENSOR * N_DP
    return (gate_out.reshape(tokens, FF), up_out.reshape(tokens, FF), total.astype(jnp.bfloat16))
```

```python
import jax
import jax.numpy as jnp
import numpy as np
from jax import lax
from jax.sharding import PartitionSpec as P

SIZES = (4, 2, 2, 4, 2)


def send(x, y=0, l=0, c=0, z=0, h=0):
    pairs = []
    for source in range(int(np.prod(SIZES))):
        place = np.unravel_index(source, SIZES)
        target = [(int(p) + d) % n for p, d, n in zip(place, (y, l, c, z, h), SIZES)]
        pairs.append((source, int(np.ravel_multi_index(target, SIZES))))
    return lax.ppermute(x, ("dp", "tensor"), pairs)


def rolled(x, axis, shift):
    n = x.shape[axis]
    return lax.dynamic_slice_in_dim(jnp.concatenate([x, x], axis), shift, n, axis)


def pick(x, axis, at):
    return lax.dynamic_index_in_dim(x, at, axis, keepdims=False)


def on_device(gate_pre, up_pre, out_grad, down_weight):
    dp, tensor = lax.axis_index("dp"), lax.axis_index("tensor")
    y, l, c = dp // 4, dp // 2 % 2, dp % 2
    z, h = tensor // 2, tensor % 2
    tokens, columns = gate_pre.shape
    half = columns // 2
    share, width = out_grad.shape
    stripe = width // 8
    shard = down_weight.shape[0]
    bf16, f32 = jnp.bfloat16, jnp.float32

    w = down_weight.reshape(shard, 4, 2, 2, half)
    w_own, w_other = pick(w, 3, c), pick(w, 3, 1 - c)
    w_core = send(w_other, c=1)
    w_both = jnp.stack([jnp.where(c == 0, w_own, w_core), jnp.where(c == 0, w_core, w_own)])
    w_both = rolled(rolled(w_both, 2, z), 3, h)
    pieces = {}
    for k in range(4):
        for j in range(2):
            part = w_both[:, :, k, j]
            pieces[(-k) % 4, j] = part if k == j == 0 else send(part, z=k, h=j)
    w_mine = jnp.stack([jnp.stack([pieces[k, j] for j in range(2)]) for k in range(4)])
    w_mine = rolled(rolled(w_mine, 0, -z % 4), 1, h)
    w_mine = w_mine.transpose(2, 0, 1, 3, 4).reshape(stripe, half)
    w_up = send(w_mine, y=-1)
    w_down = send(w_mine, y=1)
    w_far = jnp.concatenate([send(w_up[: stripe // 2], y=-1), send(w_down[stripe // 2 :], y=1)])
    w_all = jnp.concatenate([w_mine, w_up, w_far, w_down])

    o = rolled(out_grad.reshape(share, 4, 2, stripe), 1, y)
    o_own = pick(o, 2, l).reshape(share, 4 * stripe)
    o_pair = send(pick(o, 2, 1 - l).reshape(share, 4 * stripe), l=1)
    o_pair = jnp.stack([o_own, o_pair])
    o_here = jnp.stack([o_pair, send(o_pair, h=1)], axis=1)
    o_up = send(o_here, z=-1)
    o_down = send(o_here, z=1)
    o_far = jnp.stack([send(o_up[0], z=-1), send(o_down[1], z=1)])
    o_core = [o_here, o_up, o_far, o_down]
    o_all = jnp.stack(o_core + [send(x, c=1) for x in o_core], axis=1)
    o_all = o_all.reshape(2, 2 * tokens, 4 * stripe)

    def relative(x):
        x = x.reshape(4, 2, share, columns)
        return rolled(rolled(x, 0, z), 1, h).reshape(tokens, columns)

    gate, up = relative(gate_pre).astype(f32), relative(up_pre).astype(f32)
    sig = jax.nn.sigmoid(gate)
    hidden = (gate * sig * up).astype(bf16).reshape(tokens, 2, half)
    hid_own = pick(hidden, 1, c)
    hid_core = send(pick(hidden, 1, 1 - c), c=1)
    hid = jnp.concatenate([hid_own, hid_core, send(hid_own, l=1), send(hid_core, l=1)])

    hg_pair = jnp.dot(o_all[1], w_all, preferred_element_type=f32).astype(bf16)
    hg_pair = send(hg_pair, l=1)
    hg = jnp.dot(o_all[0], w_all, preferred_element_type=f32) + hg_pair.astype(f32)
    hg_own = hg[:tokens]
    hg_core = send(hg[tokens:].astype(bf16), c=1).astype(f32)
    hg = jnp.where(c == 0, jnp.concatenate([hg_own, hg_core], 1), jnp.concatenate([hg_core, hg_own], 1))
    gate_grad = (hg * up * sig * (1.0 + gate * (1.0 - sig))).astype(bf16)
    up_grad = (hg * gate * sig).astype(bf16)

    def absolute(x):
        x = x.reshape(4, 2, share, columns)
        return rolled(rolled(x, 0, -z % 4), 1, h).reshape(tokens, columns)

    factor = 1.0 / jnp.sqrt(f32(tokens * 16))
    flat = o_all.reshape(4 * tokens, 4, stripe)

    def term(k):
        product = lax.dot_general(flat[:, k], hid, (((0,), (0,)), ((), ())), preferred_element_type=f32)
        return (product * factor).astype(bf16)

    cut = stripe // 2
    far, above, below, here = term(2), term(1), term(3), term(0)
    via_down, via_up = send(far[:cut], y=1), send(far[cut:], y=-1)
    low = send(above[cut:], y=1)
    high = send(below[:cut], y=-1)
    top = send((above[:cut].astype(f32) + via_down.astype(f32)).astype(bf16), y=1)
    bottom = send((below[cut:].astype(f32) + via_up.astype(f32)).astype(bf16), y=-1)
    total = here.astype(f32) + jnp.concatenate([top, low]).astype(f32) + jnp.concatenate([high, bottom]).astype(f32)
    total = total.astype(bf16).reshape(2, cut, half)
    d_own, d_core = pick(total, 0, c), send(pick(total, 0, 1 - c), c=1)
    down_grad = jnp.where(c == 0, jnp.concatenate([d_own, d_core], 1), jnp.concatenate([d_core, d_own], 1))
    return (absolute(gate_grad), absolute(up_grad), down_grad)


def solution(mesh):
    return jax.shard_map(
        on_device,
        mesh=mesh,
        in_specs=(
            P("dp", "tensor"),
            P("dp", "tensor"),
            P(("dp", "tensor"), None),
            P(("dp", "tensor"), None),
        ),
        out_specs=(P("dp", "tensor"), P("dp", "tensor"), P("dp", "tensor")),
        check_vma=False,
    )
```

```python
import jax
import jax.numpy as jnp
import numpy as np
from jax import lax
from jax.experimental import pallas as pl
from jax.experimental.pallas import tpu as pltpu
from jax.sharding import PartitionSpec as P

SIZES = (4, 2, 2, 4, 2)
BF16, F32 = jnp.bfloat16, jnp.float32
VMEM = pl.BlockSpec(memory_space=pltpu.VMEM)
SMEM = pl.BlockSpec(memory_space=pltpu.SMEM)
EIGHT = [(k, j) for k in range(4) for j in range(2)]


def send(x, y=0, l=0, c=0, z=0, h=0):
    pairs = []
    for source in range(int(np.prod(SIZES))):
        place = np.unravel_index(source, SIZES)
        target = [(int(p) + d) % n for p, d, n in zip(place, (y, l, c, z, h), SIZES)]
        pairs.append((source, int(np.ravel_multi_index(target, SIZES))))
    return lax.ppermute(x, ("dp", "tensor"), pairs)


def call(kernel, outs, place, *args, mib=40, flops=0):
    moved = sum(a.size * a.dtype.itemsize for a in args) + sum(o.size * o.dtype.itemsize for o in outs)
    return pl.pallas_call(
        kernel,
        out_shape=outs,
        in_specs=[SMEM] + [VMEM] * len(args),
        out_specs=[VMEM] * len(outs),
        compiler_params=pltpu.CompilerParams(vmem_limit_bytes=mib << 20),
        cost_estimate=pl.CostEstimate(flops=flops, bytes_accessed=moved, transcendentals=0),
    )(place, *args)


def shape(*dims, dtype=BF16):
    return jax.ShapeDtypeStruct(dims, dtype)


def at(start, size, step=128):
    return pl.ds(pl.multiple_of(start, step), size)


def slot(place, k, j):
    return (place[3] + k) % 4 * 2 + (place[4] + j) % 2


def pack_kernel(place, grad, weight, own, other, *parts):
    y, l = place[0], place[1]
    stripe = own.shape[1] // 4
    for k in range(4):
        start = (y + k) % 4 * 2 * stripe
        to = pl.ds(k * stripe, stripe)
        own[:, to] = grad[:, at(start + l * stripe, stripe)]
        other[:, to] = grad[:, at(start + (1 - l) * stripe, stripe)]
    columns = parts[0].shape[1]
    for part, (k, j) in zip(parts, EIGHT):
        part[...] = weight[:, at(slot(place, k, j) * columns, columns)]


def weight_kernel(place, *refs):
    parts, keep, give = refs[:8], refs[8], refs[9]
    c = place[2]
    rows, half = parts[0].shape[0], keep.shape[1]
    for part, (k, j) in zip(parts, EIGHT):
        to = at(slot(place, k, j) * rows, rows, 32)
        keep[to, :] = part[:, at(c * half, half)]
        give[to, :] = part[:, at((1 - c) * half, half)]


def hidden_kernel(place, gate_ref, up_ref, own, other):
    c = place[2]
    half = own.shape[1]
    rows = own.shape[0] // 8
    for n, (k, j) in enumerate(EIGHT):
        block = at(slot(place, k, j) * rows, rows, 64)
        for out, side in ((own, c), (other, 1 - c)):
            gate = gate_ref[block, at(side * half, half)].astype(F32)
            up = up_ref[block, at(side * half, half)].astype(F32)
            out[pl.ds(n * rows, rows), :] = (gate * jax.nn.sigmoid(gate) * up).astype(BF16)


def gather_kernel(place, *refs):
    chunks, weights = refs[:16], refs[16:24]
    o_all, w_all, first, second = refs[24:]
    c = place[2]
    rows = chunks[0].shape[0] // 2
    tokens = 16 * rows
    cut = weights[0].shape[0]
    for k in range(4):
        w_all[at(k * 2 * cut + c * cut, cut, 256), :] = weights[2 * k][...]
        w_all[at(k * 2 * cut + (1 - c) * cut, cut, 256), :] = weights[2 * k + 1][...]
    for n, chunk in enumerate(chunks):
        o_all[pl.ds(n * rows, rows), :] = chunk[:rows, :]
        o_all[pl.ds(tokens + n * rows, rows), :] = chunk[rows:, :]
    tile = 256
    for out, start in ((second, tokens + tokens // 2), (first, tokens)):

        @pl.loop(0, out.shape[0] // tile)
        def _(i):
            block = o_all[at(start + i * tile, tile, tile), :]
            out[at(i * tile, tile, tile), :] = jnp.dot(
                block, w_all[...], preferred_element_type=F32
            ).astype(BF16)


def gradient_kernel(place, gate_ref, up_ref, mine_ref, pair_ref, core_ref, gate_grad, up_grad):
    c = place[2]
    half = pair_ref.shape[1]
    rows = pair_ref.shape[0] // 8
    for n, (k, j) in enumerate(EIGHT):
        block = at(slot(place, k, j) * rows, rows, 64)
        here = pl.ds(n * rows, rows)
        for side in (c, 1 - c):
            if side is c:
                grad = mine_ref[here, :] + pair_ref[here, :].astype(F32)
            else:
                grad = core_ref[here, :].astype(F32)
            columns = at(side * half, half)
            gate = gate_ref[block, columns].astype(F32)
            up = up_ref[block, columns].astype(F32)
            sig = jax.nn.sigmoid(gate)
            gate_grad[block, columns] = (grad * up * sig * (1.0 + gate * (1.0 - sig))).astype(BF16)
            up_grad[block, columns] = (grad * gate * sig).astype(BF16)


def total_kernel(place, here, top, low, high, bottom, own, other):
    c = place[2]
    cut = own.shape[0]
    for out, side in ((own, c), (other, 1 - c)):
        for s, (one, two) in enumerate(((top, high), (low, bottom))):

            @pl.when(side == s)
            def _(s=s, one=one, two=two, out=out):
                total = here[pl.ds(s * cut, cut), :].astype(F32) + one[...].astype(F32) + two[...].astype(F32)
                out[...] = total.astype(BF16)


def join_kernel(place, own, core, out):
    c = place[2]
    half = own.shape[1]
    out[:, at(c * half, half)] = own[...]
    out[:, at((1 - c) * half, half)] = core[...]


def on_device(gate_pre, up_pre, out_grad, down_weight):
    dp, tensor = lax.axis_index("dp"), lax.axis_index("tensor")
    place = jnp.stack([dp // 4, dp // 2 % 2, dp % 2, tensor // 2, tensor % 2]).astype(jnp.int32)
    tokens, columns = gate_pre.shape
    half = columns // 2
    share, width = out_grad.shape
    stripe = width // 8
    shard = down_weight.shape[0]
    cut = stripe // 2

    packed = call(
        pack_kernel,
        [shape(share, width // 2)] * 2 + [shape(shard, columns)] * 8,
        place, out_grad, down_weight,
    )
    o_own, o_other, parts = packed[0], packed[1], dict(zip(EIGHT, packed[2:]))

    came = {}
    for k, j in [(2, 1), (2, 0), (1, 1), (3, 1), (1, 0), (3, 0), (0, 1), (0, 0)]:
        came[(-k) % 4, j] = parts[k, j] if k == j == 0 else send(parts[k, j], z=k, h=j)
    o_a = jnp.concatenate([o_own, send(o_other, l=1)])
    o_b = jnp.concatenate([send(o_own, h=1), send(o_other, l=1, h=1)])

    hid_own, hid_other = call(hidden_kernel, [shape(tokens, half)] * 2, place, gate_pre, up_pre)
    hid_core = send(hid_other, c=1)
    hid_pair_own = send(hid_own, l=1)
    hid_pair_core = send(hid_core, l=1)

    keep, give = call(weight_kernel, [shape(stripe // 2, half)] * 2, place, *[came[p] for p in EIGHT])
    got = send(give, c=1)
    keep_up, keep_down = send(keep, y=-1), send(keep, y=1)
    got_up, got_down = send(got, y=-1), send(got, y=1)
    keep_far, got_far = send(keep_up, y=-1), send(got_down, y=1)
    weights = [keep, got, keep_up, got_up, keep_far, got_far, keep_down, got_down]

    a_up, a_down = send(o_a, z=-1), send(o_a, z=1)
    b_up, b_down = send(o_b, z=-1), send(o_b, z=1)
    a_far, b_far = send(a_up, z=-1), send(b_down, z=1)
    chunks = [o_a, o_b, a_up, b_up, a_far, b_far, a_down, b_down]
    chunks = chunks + [send(x, c=1) for x in chunks]

    flops = 2 * 2 * tokens * 4 * stripe * half
    o_all, w_all, first, second = call(
        gather_kernel,
        [shape(4 * tokens, 4 * stripe), shape(4 * stripe, half), shape(tokens, half), shape(tokens, half)],
        place, *chunks, *weights,
        flops=flops, mib=48,
    )
    second_in = send(second, l=1)
    first_in = send(first, l=1)

    factor = 1.0 / jnp.sqrt(F32(tokens * 16))
    hid = jnp.concatenate([hid_own, hid_core, hid_pair_own, hid_pair_core])

    def term(k):
        lhs = lax.slice_in_dim(o_all, k * stripe, (k + 1) * stripe, axis=1)
        product = lax.dot_general(lhs, hid, (((0,), (0,)), ((), ())), preferred_element_type=F32)
        return (product * factor).astype(BF16)

    far, above, below, here = term(2), term(1), term(3), term(0)
    via_down, via_up = send(far[:cut], y=1), send(far[cut:], y=-1)
    low = send(above[cut:], y=1)
    high = send(below[:cut], y=-1)
    top = send((above[:cut].astype(F32) + via_down.astype(F32)).astype(BF16), y=1)
    bottom = send((below[cut:].astype(F32) + via_up.astype(F32)).astype(BF16), y=-1)
    d_own, d_other = call(total_kernel, [shape(cut, half)] * 2, place, here, top, low, high, bottom)
    (down_grad,) = call(join_kernel, [shape(cut, columns)], place, d_own, send(d_other, c=1))

    mine = jnp.dot(o_all[: 2 * tokens], w_all, preferred_element_type=F32)
    core_out = (mine[tokens:] + second_in.astype(F32)).astype(BF16)
    gate_grad, up_grad = call(
        gradient_kernel, [shape(tokens, columns)] * 2, place,
        gate_pre, up_pre, mine[:tokens], first_in, send(core_out, c=1),
    )
    return (gate_grad, up_grad, down_grad)


def solution(mesh):
    return jax.shard_map(
        on_device,
        mesh=mesh,
        in_specs=(
            P("dp", "tensor"),
            P("dp", "tensor"),
            P(("dp", "tensor"), None),
            P(("dp", "tensor"), None),
        ),
        out_specs=(P("dp", "tensor"), P("dp", "tensor"), P("dp", "tensor")),
        check_vma=False,
    )
```

```python
import jax
import jax.numpy as jnp
import numpy as np
from jax import lax
from jax.experimental import pallas as pl
from jax.experimental.pallas import tpu as pltpu
from jax.sharding import PartitionSpec as P

SIZES = (4, 2, 2, 4, 2)
BF16, F32 = jnp.bfloat16, jnp.float32
VMEM = pl.BlockSpec(memory_space=pltpu.VMEM)
SMEM = pl.BlockSpec(memory_space=pltpu.SMEM)
EIGHT = [(k, j) for k in range(4) for j in range(2)]


def permuted(x, step):
    pairs = []
    for source in range(int(np.prod(SIZES))):
        place = [int(p) for p in np.unravel_index(source, SIZES)]
        target = [(p + d) % n for p, d, n in zip(place, step(place[2]), SIZES)]
        pairs.append((source, int(np.ravel_multi_index(target, SIZES))))
    return lax.ppermute(x, ("dp", "tensor"), pairs)


def send(x, y=0, l=0, c=0, z=0, h=0):
    return permuted(x, lambda core: (y, l, c, z, h))


def ring_y(x):
    return permuted(x, lambda core: (1 - 2 * core, 0, 0, 0, 0))


def ring_z(x):
    return permuted(x, lambda core: (0, 0, 0, 1 - 2 * core, 0))


def call(kernel, outs, place, *args, mib=40, flops=0, specs=None, grid=None, scratch=()):
    moved = sum(a.size * a.dtype.itemsize for a in args) + sum(o.size * o.dtype.itemsize for o in outs)
    whole = VMEM
    if grid is not None:
        whole = None
    specs = specs or [whole] * len(args)
    specs = [pl.BlockSpec(a.shape, lambda *_, n=a.ndim: (0,) * n) if s is None else s for s, a in zip(specs, args)]
    if grid is None:
        placed = dict(in_specs=[SMEM] + specs, out_specs=[VMEM] * len(outs), scratch_shapes=scratch)
    else:
        out_specs = [pl.BlockSpec(o.shape, lambda *_, n=len(o.shape): (0,) * n) for o in outs]
        placed = dict(
            grid_spec=pltpu.PrefetchScalarGridSpec(
                num_scalar_prefetch=1, grid=grid, in_specs=specs, out_specs=out_specs, scratch_shapes=scratch
            )
        )
    return pl.pallas_call(
        kernel,
        out_shape=outs,
        compiler_params=pltpu.CompilerParams(vmem_limit_bytes=mib << 20),
        cost_estimate=pl.CostEstimate(flops=flops, bytes_accessed=moved, transcendentals=0),
        **placed,
    )(place, *args)


def shape(*dims, dtype=BF16):
    return jax.ShapeDtypeStruct(dims, dtype)


def at(start, size, step=128):
    return pl.ds(pl.multiple_of(start, step), size)


def slot(place, k, j):
    return (place[3] + k) % 4 * 2 + (place[4] + j) % 2


def behind(place, axis, s):
    return (place[axis] + 4 + (2 * place[2] - 1) * s) % 4


def token_rows(place, n, rows):
    return at((behind(place, 3, n // 2) * 2 + (place[4] + n) % 2) * rows, rows, 64)


def pack_kernel(place, grad, weight, own, other, *parts):
    l = place[1]
    stripe = own.shape[1] // 4
    for k in range(4):
        start = k * 2 * stripe
        to = pl.ds(k * stripe, stripe)
        own[:, to] = grad[:, at(start + l * stripe, stripe)]
        other[:, to] = grad[:, at(start + (1 - l) * stripe, stripe)]
    columns = parts[0].shape[1]
    for part, (k, j) in zip(parts, EIGHT):
        part[...] = weight[:, at(slot(place, k, j) * columns, columns)]


def weight_kernel(place, *refs):
    parts, keep, give = refs[:8], refs[8], refs[9]
    c = place[2]
    rows, half = parts[0].shape[0], keep.shape[1]
    for part, (k, j) in zip(parts, EIGHT):
        to = at(slot(place, k, j) * rows, rows, 32)
        keep[to, :] = part[:, at(c * half, half)]
        give[to, :] = part[:, at((1 - c) * half, half)]


def hidden_kernel(place, gate_ref, up_ref, own, other):
    c = place[2]
    half = own.shape[1]
    rows = own.shape[0] // 8
    for n in range(8):
        block = token_rows(place, n, rows)
        for out, side in ((own, c), (other, 1 - c)):
            gate = gate_ref[block, at(side * half, half)].astype(F32)
            up = up_ref[block, at(side * half, half)].astype(F32)
            out[pl.ds(n * rows, rows), :] = (gate * jax.nn.sigmoid(gate) * up).astype(BF16)


def product_kernel(place, *refs):
    chunks, weights, out, rows_of, all_of = refs[:4], refs[4:12], refs[12], refs[13], refs[14]
    c = place[2]
    cut = weights[0].shape[0]
    for s in range(4):
        start = behind(place, 0, s) * 2 * cut
        all_of[at(start + c * cut, cut, 256), :] = weights[2 * s][...]
        all_of[at(start + (1 - c) * cut, cut, 256), :] = weights[2 * s + 1][...]
    rows = chunks[0].shape[0]
    for n in range(0, 4, 2):
        rows_of[:rows, :] = chunks[n][...]
        rows_of[rows:, :] = chunks[n + 1][...]
        product = jnp.dot(rows_of[...], all_of[...], preferred_element_type=F32)
        out[n * rows : (n + 2) * rows, :] = product.astype(out.dtype)


def term_kernel(steps, factor, place, *refs):
    chunks, (own, core, pair), outs, lhs = refs[:8], refs[8:11], refs[11:-1], refs[-1]
    step = pl.program_id(0)
    rows = chunks[0].shape[0] // 2
    tokens = 4 * rows
    for n, chunk in enumerate(chunks):
        lhs[pl.ds(n * rows, rows), :] = chunk[:rows, :]
        lhs[pl.ds(2 * tokens + n * rows, rows), :] = chunk[rows:, :]

    def part(start, size, rhs):
        return lax.dot_general(
            lhs[start : start + size, :], rhs[...], (((0,), (0,)), ((), ())), preferred_element_type=F32
        )

    product = part(0, tokens, own) + part(tokens, tokens, core) + part(2 * tokens, 2 * tokens, pair)
    product = (product * factor).astype(BF16)
    for n, out in enumerate(outs):

        @pl.when(step == n)
        def _(out=out):
            out[...] = product


def gradient_kernel(place, gate_ref, up_ref, mine_a, mine_b, pair_a, pair_b, core_ref, gate_grad, up_grad):
    c = place[2]
    half = core_ref.shape[1]
    rows = core_ref.shape[0] // 8
    for n in range(8):
        block = token_rows(place, n, rows)
        here = pl.ds(n * rows, rows)
        part = pl.ds(n % 4 * rows, rows)
        mine, pair = (mine_a, pair_a) if n < 4 else (mine_b, pair_b)
        for side, grad in (
            (c, mine[part, :] + pair[part, :].astype(F32)),
            (1 - c, core_ref[here, :].astype(F32)),
        ):
            columns = at(side * half, half)
            gate = gate_ref[block, columns].astype(F32)
            up = up_ref[block, columns].astype(F32)
            sig = jax.nn.sigmoid(gate)
            gate_grad[block, columns] = (grad * up * sig * (1.0 + gate * (1.0 - sig))).astype(BF16)
            up_grad[block, columns] = (grad * gate * sig).astype(BF16)


def join_kernel(place, mine, came, core, out):
    c = place[2]
    half = core.shape[1]
    out[:, at(c * half, half)] = (mine[...].astype(F32) + came[...].astype(F32)).astype(BF16)
    out[:, at((1 - c) * half, half)] = core[...]


def added(a, b):
    return (a.astype(F32) + b.astype(F32)).astype(BF16)


def on_device(gate_pre, up_pre, out_grad, down_weight):
    dp, tensor = lax.axis_index("dp"), lax.axis_index("tensor")
    place = jnp.stack([dp // 4, dp // 2 % 2, dp % 2, tensor // 2, tensor % 2]).astype(jnp.int32)
    tokens, columns = gate_pre.shape
    half = columns // 2
    share, width = out_grad.shape
    stripe = width // 8
    shard = down_weight.shape[0]
    cut = stripe // 2

    packed = call(
        pack_kernel,
        [shape(share, width // 2)] * 2 + [shape(shard, columns)] * 8,
        place, out_grad, down_weight,
    )
    o_own, o_other, parts = packed[0], packed[1], dict(zip(EIGHT, packed[2:]))

    o_here = jnp.concatenate([o_own, send(o_own, h=1), send(o_other, l=1), send(o_other, l=1, h=1)])
    came = {}
    for k, j in [(2, 1), (1, 1), (3, 1), (0, 1), (2, 0), (1, 0), (3, 0), (0, 0)]:
        came[(-k) % 4, j] = parts[k, j] if k == j == 0 else send(parts[k, j], z=k, h=j)

    hid_own, hid_other = call(hidden_kernel, [shape(tokens, half)] * 2, place, gate_pre, up_pre)
    hid_core = send(hid_other, c=1)
    hid_pair = send(jnp.concatenate([hid_own, hid_core]), l=1)

    keep, give = call(weight_kernel, [shape(cut, half)] * 2, place, *[came[p] for p in EIGHT])
    got = send(give, c=1)
    weights = [keep, got]
    for _ in range(3):
        weights += [ring_y(weights[-2]), ring_y(weights[-1])]

    chunks = [o_here]
    for _ in range(3):
        chunks.append(ring_z(chunks[-1]))
    cores = [send(x, c=1) for x in chunks]

    def hidden_grad(first, side, dtype):
        picked = chunks[first : first + 2] + cores[first : first + 2]
        rows = 2 * share
        specs = [pl.BlockSpec((rows, width // 2), lambda *_: (side, 0))] * 4 + [None] * 8
        return call(
            product_kernel, [shape(4 * rows, half, dtype=dtype)], place, *picked, *weights,
            specs=specs, grid=(1,), flops=2 * 4 * rows * 4 * stripe * half,
            scratch=[pltpu.VMEM((2 * rows, width // 2), BF16), pltpu.VMEM((width // 2, half), BF16)],
        )[0]

    pair_a = send(hidden_grad(0, 1, BF16), l=1)
    pair_b = send(hidden_grad(2, 1, BF16), l=1)

    factor = 1.0 / float(np.sqrt(np.float32(tokens * 16)))

    def terms(steps):
        def block(i, place):
            s = steps[0]
            for n in range(1, len(steps)):
                s = jnp.where(i // 2 == n, steps[n], s)
            return 0, behind(place, 0, s) * 2 + (1 - place[2] + i) % 2

        specs = [pl.BlockSpec((4 * share, cut), block)] * 8 + [None] * 3

        def kernel(*refs):
            term_kernel(steps, factor, *refs)

        return call(
            kernel, [shape(cut, half)] * (2 * len(steps)), place, *chunks, *cores, hid_own, hid_core, hid_pair,
            specs=specs, grid=(2 * len(steps),), flops=4 * len(steps) * 4 * tokens * cut * half,
            scratch=[pltpu.VMEM((4 * tokens, cut), BF16)],
        )

    other_1, own_1 = terms([1])
    other_2, own_2, other_3, own_3, other_0, own_0 = terms([2, 3, 0])
    other = ring_y(added(other_3, ring_y(added(other_2, ring_y(other_1)))))
    own = ring_y(added(own_3, ring_y(added(own_2, ring_y(own_1)))))
    d_core = send(added(other_0, other), c=1)
    (down_grad,) = call(join_kernel, [shape(cut, columns)], place, own_0, own, d_core)

    mine_a, mine_b = hidden_grad(0, 0, F32), hidden_grad(2, 0, F32)
    core_out = jnp.concatenate(
        [(m[tokens // 2 :] + p[tokens // 2 :].astype(F32)).astype(BF16) for m, p in ((mine_a, pair_a), (mine_b, pair_b))]
    )
    gate_grad, up_grad = call(
        gradient_kernel, [shape(tokens, columns)] * 2, place,
        gate_pre, up_pre, mine_a, mine_b, pair_a, pair_b, send(core_out, c=1),
    )
    return (gate_grad, up_grad, down_grad)


def solution(mesh):
    return jax.shard_map(
        on_device,
        mesh=mesh,
        in_specs=(
            P("dp", "tensor"),
            P("dp", "tensor"),
            P(("dp", "tensor"), None),
            P(("dp", "tensor"), None),
        ),
        out_specs=(P("dp", "tensor"), P("dp", "tensor"), P("dp", "tensor")),
        check_vma=False,
    )
```

```python
import jax
import jax.numpy as jnp
import numpy as np
from jax import lax
from jax.experimental import pallas as pl
from jax.experimental.pallas import tpu as pltpu
from jax.sharding import PartitionSpec as P

SIZES = (4, 2, 2, 4, 2)
BF16, F32 = jnp.bfloat16, jnp.float32
VMEM = pl.BlockSpec(memory_space=pltpu.VMEM)
SMEM = pl.BlockSpec(memory_space=pltpu.SMEM)
EIGHT = [(k, j) for k in range(4) for j in range(2)]


def permuted(x, step):
    pairs = []
    for source in range(int(np.prod(SIZES))):
        place = [int(p) for p in np.unravel_index(source, SIZES)]
        target = [(p + d) % n for p, d, n in zip(place, step(place[2]), SIZES)]
        pairs.append((source, int(np.ravel_multi_index(target, SIZES))))
    return lax.ppermute(x, ("dp", "tensor"), pairs)


def send(x, y=0, l=0, c=0, z=0, h=0):
    return permuted(x, lambda core: (y, l, c, z, h))


def ring_y(x):
    return permuted(x, lambda core: (1 - 2 * core, 0, 0, 0, 0))


def ring_z(x):
    return permuted(x, lambda core: (0, 0, 0, 1 - 2 * core, 0))


def call(kernel, outs, place, *args, mib=40, flops=0, specs=None, grid=None, scratch=()):
    moved = sum(a.size * a.dtype.itemsize for a in args) + sum(o.size * o.dtype.itemsize for o in outs)
    whole = VMEM
    if grid is not None:
        whole = None
    specs = specs or [whole] * len(args)
    specs = [pl.BlockSpec(a.shape, lambda *_, n=a.ndim: (0,) * n) if s is None else s for s, a in zip(specs, args)]
    if grid is None:
        placed = dict(in_specs=[SMEM] + specs, out_specs=[VMEM] * len(outs), scratch_shapes=scratch)
    else:
        out_specs = [pl.BlockSpec(o.shape, lambda *_, n=len(o.shape): (0,) * n) for o in outs]
        placed = dict(
            grid_spec=pltpu.PrefetchScalarGridSpec(
                num_scalar_prefetch=1, grid=grid, in_specs=specs, out_specs=out_specs, scratch_shapes=scratch
            )
        )
    return pl.pallas_call(
        kernel,
        out_shape=outs,
        compiler_params=pltpu.CompilerParams(vmem_limit_bytes=mib << 20),
        cost_estimate=pl.CostEstimate(flops=flops, bytes_accessed=moved, transcendentals=0),
        **placed,
    )(place, *args)


def shape(*dims, dtype=BF16):
    return jax.ShapeDtypeStruct(dims, dtype)


def at(start, size, step=128):
    return pl.ds(pl.multiple_of(start, step), size)


def slot(place, k, j):
    return (place[3] + k) % 4 * 2 + (place[4] + j) % 2


def behind(place, axis, s):
    return (place[axis] + 4 + (2 * place[2] - 1) * s) % 4


def token_rows(place, n, rows):
    return at((behind(place, 3, n // 2) * 2 + (place[4] + n) % 2) * rows, rows, 64)


def pack_kernel(place, grad, weight, own, other, *parts):
    l = place[1]
    stripe = own.shape[1] // 4
    for k in range(4):
        start = k * 2 * stripe
        to = pl.ds(k * stripe, stripe)
        own[:, to] = grad[:, at(start + l * stripe, stripe)]
        other[:, to] = grad[:, at(start + (1 - l) * stripe, stripe)]
    columns = parts[0].shape[1]
    for part, (k, j) in zip(parts, EIGHT):
        part[...] = weight[:, at(slot(place, k, j) * columns, columns)]


def weight_kernel(place, *refs):
    parts, keep, give = refs[:8], refs[8], refs[9]
    c = place[2]
    rows, half = parts[0].shape[0], keep.shape[1]
    for part, (k, j) in zip(parts, EIGHT):
        to = at(slot(place, k, j) * rows, rows, 32)
        keep[to, :] = part[:, at(c * half, half)]
        give[to, :] = part[:, at((1 - c) * half, half)]


def hidden_kernel(place, gate_ref, up_ref, own, other):
    c = place[2]
    half = own.shape[1]
    rows = own.shape[0] // 8
    for n in range(8):
        block = token_rows(place, n, rows)
        for out, side in ((own, c), (other, 1 - c)):
            gate = gate_ref[block, at(side * half, half)].astype(F32)
            up = up_ref[block, at(side * half, half)].astype(F32)
            out[pl.ds(n * rows, rows), :] = (gate * jax.nn.sigmoid(gate) * up).astype(BF16)


def product_kernel(place, *refs):
    chunks, weights, out, rows_of, all_of = refs[:8], refs[8:16], refs[16], refs[17], refs[18]
    c = place[2]
    cut = weights[0].shape[0]
    for s in range(4):
        start = behind(place, 0, s) * 2 * cut
        all_of[at(start + c * cut, cut, 256), :] = weights[2 * s][...]
        all_of[at(start + (1 - c) * cut, cut, 256), :] = weights[2 * s + 1][...]
    rows = chunks[0].shape[0]
    for n in range(0, 8, 4):
        for m in range(4):
            rows_of[m * rows : (m + 1) * rows, :] = chunks[n + m][...]
        product = jnp.dot(rows_of[...], all_of[...], preferred_element_type=F32)
        out[n * rows : (n + 4) * rows, :] = product.astype(out.dtype)


def term_kernel(steps, factor, place, *refs):
    chunks, rights, outs, lhs = refs[:16], refs[16:21], refs[21:-1], refs[-1]
    step = pl.program_id(0)
    rows = chunks[0].shape[0] // 2
    tokens = 8 * rows
    for n, chunk in enumerate(chunks):
        to = n // 8 * tokens + (n % 4 * 2 + n // 4 % 2) * rows
        lhs[pl.ds(to, rows), :] = chunk[:rows, :]
        lhs[pl.ds(2 * tokens + to, rows), :] = chunk[rows:, :]

    product, start = None, 0
    for right in rights:
        stop = start + right.shape[0]
        part = lax.dot_general(
            lhs[start:stop, :], right[...], (((0,), (0,)), ((), ())), preferred_element_type=F32
        )
        product, start = part if product is None else product + part, stop
    product = (product * factor).astype(BF16)
    for n, out in enumerate(outs):

        @pl.when(step == n)
        def _(out=out):
            out[...] = product


def gradient_kernel(place, gate_ref, up_ref, mine_a, mine_b, pair_a, pair_b, core_ref, gate_grad, up_grad):
    c = place[2]
    half = core_ref.shape[1]
    rows = core_ref.shape[0] // 8
    for n in range(8):
        block = token_rows(place, n, rows)
        here = pl.ds(n * rows, rows)
        part = pl.ds(n % 4 * rows, rows)
        mine, pair = (mine_a, pair_a) if n < 4 else (mine_b, pair_b)
        for side, grad in (
            (c, mine[part, :] + pair[part, :].astype(F32)),
            (1 - c, core_ref[here, :].astype(F32)),
        ):
            columns = at(side * half, half)
            gate = gate_ref[block, columns].astype(F32)
            up = up_ref[block, columns].astype(F32)
            sig = jax.nn.sigmoid(gate)
            gate_grad[block, columns] = (grad * up * sig * (1.0 + gate * (1.0 - sig))).astype(BF16)
            up_grad[block, columns] = (grad * gate * sig).astype(BF16)


def join_kernel(place, mine, came, core, out):
    c = place[2]
    half = core.shape[1]
    out[:, at(c * half, half)] = (mine[...].astype(F32) + came[...].astype(F32)).astype(BF16)
    out[:, at((1 - c) * half, half)] = core[...]


def tied(x, *first):
    return lax.optimization_barrier((x, first))[0]


def added(a, b):
    return (a.astype(F32) + b.astype(F32)).astype(BF16)


def on_device(gate_pre, up_pre, out_grad, down_weight):
    dp, tensor = lax.axis_index("dp"), lax.axis_index("tensor")
    place = jnp.stack([dp // 4, dp // 2 % 2, dp % 2, tensor // 2, tensor % 2]).astype(jnp.int32)
    tokens, columns = gate_pre.shape
    half = columns // 2
    share, width = out_grad.shape
    stripe = width // 8
    shard = down_weight.shape[0]
    cut = stripe // 2

    packed = call(
        pack_kernel,
        [shape(share, width // 2)] * 2 + [shape(shard, columns)] * 8,
        place, out_grad, down_weight,
    )
    o_own, o_other, parts = packed[0], packed[1], dict(zip(EIGHT, packed[2:]))

    o_pair = send(o_other, l=1)
    came = {(0, 0): parts[0, 0]}
    for k, j in [(2, 0), (2, 1), (1, 0), (3, 0), (1, 1), (3, 1), (0, 1)]:
        came[(-k) % 4, j] = send(parts[k, j], z=k, h=j)
    o_near = tied(jnp.concatenate([o_own, o_pair]), came[2, 0], came[2, 1])
    o_far = jnp.concatenate([send(o_own, h=1), send(o_other, l=1, h=1)])

    hid_own, hid_other = call(hidden_kernel, [shape(tokens, half)] * 2, place, gate_pre, up_pre)
    hid_core = send(hid_other, c=1)
    hid_pair_own = send(hid_own, l=1)
    hid_pair_core = [send(hid_core[:cut], l=1), send(hid_core[cut:], l=1)]

    arrived = tied([came[p] for p in EIGHT], hid_core)
    keep, give = call(weight_kernel, [shape(cut, half)] * 2, place, *arrived)
    keep, got, near, far = [keep], [send(give, c=1)], [o_near], [o_far]
    near.append(ring_z(near[0]))
    far.append(ring_z(far[0]))
    for s in range(3):
        keep.append(ring_y(keep[s]))
        got.append(ring_y(got[s]))
    near.append(ring_z(tied(near[1], keep[0])))
    far.append(ring_z(tied(far[1], got[0])))
    near.append(ring_z(tied(near[2], keep[1], hid_pair_own)))
    far.append(ring_z(tied(far[2], got[1])))
    weights = [w for pair in zip(keep, got) for w in pair]
    chunks = near + far
    last = tied(near[3], keep[2], hid_pair_core[0]), tied(far[3], got[2], hid_pair_core[1])
    cores = [send(x, c=1) for x in near[:3] + [last[0]] + far[:3] + [last[1]]]

    def hidden_grad(first, side, dtype, *after):
        picked = [x[n + f] for x in (chunks, cores) for n in (first, first + 1) for f in (0, 4)]
        rows = 2 * share
        specs = [pl.BlockSpec((share, width // 2), lambda *_: (side, 0))] * 8 + [None] * 8
        return call(
            product_kernel, [shape(4 * rows, half, dtype=dtype)], place, *tied(picked, *after), *weights,
            specs=specs, grid=(1,), flops=2 * 4 * rows * 4 * stripe * half,
            scratch=[pltpu.VMEM((4 * share, width // 2), BF16), pltpu.VMEM((width // 2, half), BF16)],
        )[0]

    factor = 1.0 / float(np.sqrt(np.float32(tokens * 16)))

    def terms(steps, *after):
        def block(i, place):
            s = steps[0]
            for n in range(1, len(steps)):
                s = jnp.where(i // 2 == n, steps[n], s)
            return 0, behind(place, 0, s) * 2 + (1 - place[2] + i) % 2

        specs = [pl.BlockSpec((2 * share, cut), block)] * 16 + [None] * 5

        def kernel(*refs):
            term_kernel(steps, factor, *refs)

        return call(
            kernel, [shape(cut, half)] * (2 * len(steps)), place, *tied(chunks + cores, *after),
            hid_own, hid_core, hid_pair_own, *hid_pair_core,
            specs=specs, grid=(2 * len(steps),), flops=4 * len(steps) * 4 * tokens * cut * half,
            scratch=[pltpu.VMEM((4 * tokens, cut), BF16)],
        )

    pair_a = hidden_grad(0, 1, BF16)
    other_1, own_1 = terms([1], pair_a)
    pair_b = hidden_grad(2, 1, BF16, other_1)
    other_2, own_2 = terms([2], pair_b)
    mine_a = hidden_grad(0, 0, F32, other_2)
    other_3, own_3 = terms([3], mine_a)
    mine_b = hidden_grad(2, 0, F32, other_3)
    other_0, own_0 = terms([0], mine_b)
    pair_a, pair_b = send(pair_a, l=1), send(pair_b, l=1)
    other = ring_y(added(other_3, ring_y(added(other_2, ring_y(other_1)))))
    own = ring_y(added(own_3, ring_y(added(own_2, ring_y(own_1)))))
    d_core = send(added(other_0, other), c=1)
    (down_grad,) = call(join_kernel, [shape(cut, columns)], place, own_0, own, d_core)
    core_out = jnp.concatenate(
        [(m[tokens // 2 :] + p[tokens // 2 :].astype(F32)).astype(BF16) for m, p in ((mine_a, pair_a), (mine_b, pair_b))]
    )
    gate_grad, up_grad = call(
        gradient_kernel, [shape(tokens, columns)] * 2, place,
        gate_pre, up_pre, mine_a, mine_b, pair_a, pair_b, send(core_out, c=1),
    )
    return (gate_grad, up_grad, down_grad)


def solution(mesh):
    return jax.shard_map(
        on_device,
        mesh=mesh,
        in_specs=(
            P("dp", "tensor"),
            P("dp", "tensor"),
            P(("dp", "tensor"), None),
            P(("dp", "tensor"), None),
        ),
        out_specs=(P("dp", "tensor"), P("dp", "tensor"), P("dp", "tensor")),
        check_vma=False,
    )
```

```python
import jax
import jax.numpy as jnp
import numpy as np
from jax import lax
from jax.experimental import pallas as pl
from jax.experimental.pallas import tpu as pltpu
from jax.sharding import PartitionSpec as P

SIZES = (4, 2, 2, 4, 2)
BF16, F32 = jnp.bfloat16, jnp.float32
VMEM = pl.BlockSpec(memory_space=pltpu.VMEM)
SMEM = pl.BlockSpec(memory_space=pltpu.SMEM)
EIGHT = [(k, j) for k in range(4) for j in range(2)]


def permuted(x, step):
    pairs = []
    for source in range(int(np.prod(SIZES))):
        place = [int(p) for p in np.unravel_index(source, SIZES)]
        target = [(p + d) % n for p, d, n in zip(place, step(place[2]), SIZES)]
        pairs.append((source, int(np.ravel_multi_index(target, SIZES))))
    return lax.ppermute(x, ("dp", "tensor"), pairs)


def send(x, y=0, l=0, c=0, z=0, h=0):
    return permuted(x, lambda core: (y, l, c, z, h))


def ring_y(x):
    return permuted(x, lambda core: (1 - 2 * core, 0, 0, 0, 0))


def ring_z(x):
    return permuted(x, lambda core: (0, 0, 0, 1 - 2 * core, 0))


def call(kernel, outs, place, *args, mib=24, specs=None, grid=None, to=None, scratch=(), us=0.0, alias=None):
    specs, to = specs or [VMEM] * len(args), to or [VMEM] * len(outs)
    if grid is None:
        placed = dict(in_specs=[SMEM] + specs, out_specs=to, scratch_shapes=scratch)
    else:
        placed = dict(
            grid_spec=pltpu.PrefetchScalarGridSpec(
                num_scalar_prefetch=1, grid=grid, in_specs=specs, out_specs=to, scratch_shapes=scratch
            )
        )
    return pl.pallas_call(
        kernel,
        out_shape=outs,
        input_output_aliases=alias or {},
        compiler_params=pltpu.CompilerParams(vmem_limit_bytes=mib << 20),
        cost_estimate=pl.CostEstimate(flops=int(us * 1.1e9), bytes_accessed=0, transcendentals=0),
        **placed,
    )(place, *args)


def shape(*dims, dtype=BF16):
    return jax.ShapeDtypeStruct(dims, dtype)


def at(start, size, step=128):
    return pl.ds(pl.multiple_of(start, step), size)


def slot(place, k, j):
    return (place[3] + k) % 4 * 2 + (place[4] + j) % 2


def behind(place, axis, s):
    return (place[axis] + 4 + (2 * place[2] - 1) * s) % 4


def chunk_rows(place, s, rows):
    return at((4 + (2 * place[2] - 1) * s) % 4 * rows, rows, 128)


def pack_kernel(place, grad, weight, own, other, *parts):
    l, c = place[1], place[2]
    stripe = own.shape[1] // 8
    for out, side in ((own, l), (other, 1 - l)):
        for i, core in enumerate((c, 1 - c)):
            for k in range(4):
                to = pl.ds((i * 4 + k) * stripe, stripe)
                out[:, to] = grad[:, at((k * 4 + side * 2 + core) * stripe, stripe)]
    rows, columns = weight.shape[0], parts[0].shape[1]
    for n, (k, j) in enumerate(EIGHT):
        parts[k][j * rows : (j + 1) * rows, :] = weight[:, at(slot(place, k, j) * columns, columns)]


def split_kernel(place, *refs):
    parts, (keep, give) = refs[:4], refs[4:]
    rows, quarter = parts[0].shape[0], keep.shape[1]
    for n, part in enumerate(parts):
        keep[n * rows : (n + 1) * rows, :] = part[:, :quarter]
        give[n * rows : (n + 1) * rows, :] = part[:, quarter:]


def weight_kernel(place, *refs):
    parts, outs = refs[:4], refs[4:]
    rows = parts[0].shape[0] // 2
    for k, part in enumerate(parts):
        to = at((place[3] + k) % 4 * rows, rows, 32)
        for j, out in enumerate(outs):
            out[to, :] = part[j * rows : (j + 1) * rows, :]


def hidden_kernel(place, gate_ref, up_ref, out):
    gate, up = gate_ref[...].astype(F32), up_ref[...].astype(F32)
    out[...] = (gate * jax.nn.sigmoid(gate) * up).astype(BF16)


def product_kernel(l, columns, count, place, *refs):
    chunks, weights, more, outs, (rows_of, all_of) = refs[:4], refs[4:12], refs[12 : -2 - count], refs[-2 - count : -2], refs[-2:]
    rows, cut = chunks[0].shape[0] // 2, weights[0].shape[0] // 4
    for s in range(4):
        rows_of[chunk_rows(place, s, rows), :] = chunks[s][l * rows : (l + 1) * rows, :]
        for j in range(2):
            for z in range(4):
                to = ((behind(place, 0, s) * 4 + z) * 2 + (place[4] + j) % 2) * cut
                all_of[at(to, cut, 32), :] = weights[4 * j + s][z * cut : (z + 1) * cut, columns]
    half = weights[0].shape[1] // 2
    for i in range(all_of.shape[1] // half):
        part = slice(i * half, (i + 1) * half)
        product = jnp.dot(rows_of[...], all_of[:, part], preferred_element_type=F32)
        if more:
            product = product + more[i][...].astype(F32)
        if count == 1:
            outs[0][:, part] = product.astype(outs[0].dtype)
        else:
            outs[i][...] = product.astype(outs[i].dtype)


def term_kernel(s, factor, place, *refs):
    chunks, rights, outs, lhs = refs[:8], refs[8:12], refs[12:14], refs[14]
    rows = chunks[0].shape[0] // 2
    cut, half = outs[0].shape
    block = at(behind(place, 0, s) * cut, cut, 256)
    for n, chunk in enumerate(chunks):
        to = chunk_rows(place, n % 4, rows)
        for l in range(2):
            lhs[2 * l + n // 4, to, :] = chunk[l * rows : (l + 1) * rows, block]
    for i, out in enumerate(outs):
        product = None
        for n, right in enumerate(rights):
            right = right[:, i * half : (i + 1) * half]
            part = lax.dot_general(lhs[n], right, (((0,), (0,)), ((), ())), preferred_element_type=F32)
            product = part if product is None else product + part
        out[...] = (product * factor).astype(BF16)


def chip_kernel(place, *refs):
    half, start = refs[0].shape[1], 0
    for out in refs[4:]:
        rows = slice(start, start + out.shape[0])
        for i in range(2):
            total = refs[i][rows, :] + refs[2 + i][rows, :].astype(F32)
            out[:, i * half : (i + 1) * half] = total.astype(BF16)
        start = rows.stop


def gradient_kernel(first, sizes, place, *refs):
    pieces = len(sizes)
    gate_hbm, up_hbm, mine = refs[:3]
    sums = refs[3 : 3 + pieces]
    outs_hbm, (loaded, stored, load_sem, store_sem) = refs[-6:-4], refs[-4:]
    rows = mine.shape[0] // 8
    at_block = []
    for piece, size in zip(sums, sizes):
        at_block += [(piece, n) for n in range(size)]
    blocks = [at(slot(place, *EIGHT[first + n]) * rows, rows, 64) for n in range(len(at_block))]
    loads, stores = [], []
    for n, block in enumerate(blocks):
        for i, ref in enumerate((gate_hbm, up_hbm)):
            loads.append(pltpu.make_async_copy(ref.at[block, :], loaded.at[n, i], load_sem.at[n, i]))
            loads[-1].start()
    for n, block in enumerate(blocks):
        piece, m = at_block[n]
        grad = mine[(first + n) * rows : (first + n + 1) * rows, :] + piece[m * rows : (m + 1) * rows, :].astype(F32)
        for load in loads[2 * n : 2 * n + 2]:
            load.wait()
        gate, up = loaded[n, 0].astype(F32), loaded[n, 1].astype(F32)
        sig = jax.nn.sigmoid(gate)
        stored[n, 0] = (grad * up * sig * (1.0 + gate * (1.0 - sig))).astype(BF16)
        stored[n, 1] = (grad * gate * sig).astype(BF16)
        for i, ref in enumerate(outs_hbm):
            stores.append(pltpu.make_async_copy(stored.at[n, i], ref.at[block, :], store_sem.at[n, i]))
            stores[-1].start()
    for store in stores:
        store.wait()


def join_kernel(place, *refs):
    half = refs[0].shape[1]
    for i in range(2):
        total = refs[i][...].astype(F32) + refs[2 + i][...].astype(F32)
        refs[4][:, i * half : (i + 1) * half] = total.astype(BF16)


def tied(x, *first):
    return lax.optimization_barrier((x, first))[0]


def added(a, b):
    return (a.astype(F32) + b.astype(F32)).astype(BF16)


def on_device(gate_pre, up_pre, out_grad, down_weight):
    dp, tensor = lax.axis_index("dp"), lax.axis_index("tensor")
    place = jnp.stack([dp // 4, dp // 2 % 2, dp % 2, tensor // 2, tensor % 2]).astype(jnp.int32)
    tokens, columns = gate_pre.shape
    half = columns // 2
    share, width = out_grad.shape
    quarter = width // 4
    cut = quarter // 4
    shard = down_weight.shape[0]

    packed = call(
        pack_kernel, [shape(share, 2 * quarter)] * 2 + [shape(2 * shard, columns)] * 4, place, out_grad, down_weight
    )
    o_own, o_other, parts = packed[0], packed[1], packed[2:]

    parts = [parts[0]] + [send(parts[4 - k], z=4 - k) for k in (1, 2, 3)]
    near, give = call(weight_kernel, [shape(4 * shard, columns)] * 2, place, *parts)
    near, far = [near], [send(give, h=1)]
    o_l, o_h, o_lh = send(o_other, l=1), send(o_own, h=1), send(o_other, l=1, h=1)
    own, give = call(split_kernel, [shape(4 * share, quarter)] * 2, place, o_own, o_h, o_l, o_lh)

    block = pl.BlockSpec((share, columns), lambda n, place: (slot(place, n // 2, n % 2), 0))
    there = pl.BlockSpec((share, columns), lambda n, place: (n, 0))
    (hid_own,) = call(
        hidden_kernel, [shape(tokens, columns)], place, *tied((gate_pre, up_pre), o_own),
        specs=[block] * 2, grid=(8,), to=[there],
    )
    hid_core = send(hid_own, c=1)
    hid_pair = send(tied(hid_own, far[0], o_h, o_l, o_lh), l=1)

    near.append(ring_y(near[0]))
    own, core = [own], [send(give, c=1)]
    own.append(ring_z(own[0]))
    core.append(ring_z(core[0]))
    far.append(ring_y(far[0]))
    near.append(ring_y(near[1]))
    own.append(ring_z(tied(own[1], near[2])))
    core.append(ring_z(tied(core[1], far[1])))
    far.append(ring_y(far[1]))
    near.append(ring_y(near[2]))
    own.append(ring_z(tied(own[2], near[3])))
    core.append(ring_z(tied(core[2], far[2])))
    far.append(ring_y(far[2]))
    weights = near + far
    hid_last = send(tied(hid_pair, hid_core, own[3], core[3], far[3]), c=1)

    def hidden_grad(l, c, side, outs, *after, more=()):
        wide = slice(0, columns) if side is None else slice(side * half, (side + 1) * half)
        size = wide.stop - wide.start

        def kernel(*refs):
            product_kernel(l, wide, len(outs), *refs)

        return call(
            kernel, outs, place, *tied((own, core)[c], *after), *weights, *more,
            us=size / half * 1.6, scratch=[pltpu.VMEM((tokens, quarter), BF16), pltpu.VMEM((quarter, size), BF16)],
        )

    factor = 1.0 / float(np.sqrt(np.float32(tokens * 16)))

    def term(s, *after):
        def kernel(*refs):
            term_kernel(s, factor, *refs)

        return call(
            kernel, [shape(cut, half)] * 2, place, *tied(own + core, *after), hid_own, hid_core, hid_pair, hid_last,
            us=3.1, scratch=[pltpu.VMEM((4, tokens, cut), BF16)],
        )

    out, wide = [shape(tokens, half)], [shape(tokens, half, dtype=F32)]
    out_0 = hidden_grad(1, 1, 0, out)[0]
    pair_0 = hidden_grad(1, 0, 0, wide, out_0)[0]
    out_1 = hidden_grad(1, 1, 1, out, pair_0)[0]
    pair_1 = hidden_grad(1, 0, 1, wide, out_1)[0]
    out_0, out_1 = send(out_0, c=1), send(out_1, c=1)
    sizes = [6, 2]
    pairs = call(chip_kernel, [shape(n * share, columns) for n in sizes], place, pair_0, pair_1, out_0, out_1)
    first = term(1, pairs[0])
    second = term(2, first[0])
    core_out = [send(x, c=1) for x in hidden_grad(0, 1, None, out * 2, second[0])]
    first = [ring_y(x) for x in first]
    second = [ring_y(added(a, b)) for a, b in zip(second, first)]
    third = term(3, first[0])
    (mine,) = hidden_grad(0, 0, None, [shape(tokens, columns, dtype=F32)], third[0], second[0], more=core_out)
    third = [ring_y(added(a, b)) for a, b in zip(third, second)]
    pairs = [send(x, l=1) for x in pairs]
    def gradients(first, pieces, mine, before=()):
        def kernel(*refs):
            gradient_kernel(first, [p.shape[0] // share for p in pieces], *refs)

        count = sum(p.shape[0] for p in pieces) // share
        hbm = pl.BlockSpec(memory_space=pltpu.HBM)
        return call(
            kernel, [shape(tokens, columns)] * 2, place, gate_pre, up_pre, mine, *pieces, *before,
            specs=[hbm] * 2 + [VMEM] * (1 + len(pieces)) + [hbm] * len(before), to=[hbm] * 2,
            alias={4 + len(pieces) + i: i for i in range(len(before))},
            scratch=[pltpu.VMEM((count, 2, share, columns), BF16)] * 2 + [pltpu.SemaphoreType.DMA((count, 2))] * 2,
        )

    gradient = gradients(0, pairs[:1], mine)
    last = term(0, gradient[0])
    (down_grad,) = call(join_kernel, [shape(cut, columns)], place, *last, *third)
    gate_grad, up_grad = gradients(sizes[0], pairs[1:], mine, gradient)
    return (gate_grad, up_grad, down_grad)


def solution(mesh):
    return jax.shard_map(
        on_device,
        mesh=mesh,
        in_specs=(
            P("dp", "tensor"),
            P("dp", "tensor"),
            P(("dp", "tensor"), None),
            P(("dp", "tensor"), None),
        ),
        out_specs=(P("dp", "tensor"), P("dp", "tensor"), P("dp", "tensor")),
        check_vma=False,
    )
```

```python
import jax
import jax.numpy as jnp
import numpy as np
from jax import lax
from jax.experimental import pallas as pl
from jax.experimental.pallas import tpu as pltpu
from jax.sharding import PartitionSpec as P

SIZES = (4, 2, 2, 4, 2)
BF16, F32 = jnp.bfloat16, jnp.float32
VMEM = pl.BlockSpec(memory_space=pltpu.VMEM)
SMEM = pl.BlockSpec(memory_space=pltpu.SMEM)
EIGHT = [(k, j) for k in range(4) for j in range(2)]


def permuted(x, step):
    pairs = []
    for source in range(int(np.prod(SIZES))):
        place = [int(p) for p in np.unravel_index(source, SIZES)]
        target = [(p + d) % n for p, d, n in zip(place, step(place[2]), SIZES)]
        pairs.append((source, int(np.ravel_multi_index(target, SIZES))))
    return lax.ppermute(x, ("dp", "tensor"), pairs)


def send(x, y=0, l=0, c=0, z=0, h=0):
    return permuted(x, lambda core: (y, l, c, z, h))


def ring_y(x):
    return permuted(x, lambda core: (1 - 2 * core, 0, 0, 0, 0))


def ring_z(x):
    return permuted(x, lambda core: (0, 0, 0, 1 - 2 * core, 0))


def call(kernel, outs, place, *args, mib=24, specs=None, grid=None, to=None, scratch=(), us=0.0, alias=None):
    specs, to = specs or [VMEM] * len(args), to or [VMEM] * len(outs)
    if grid is None:
        placed = dict(in_specs=[SMEM] + specs, out_specs=to, scratch_shapes=scratch)
    else:
        placed = dict(
            grid_spec=pltpu.PrefetchScalarGridSpec(
                num_scalar_prefetch=1, grid=grid, in_specs=specs, out_specs=to, scratch_shapes=scratch
            )
        )
    return pl.pallas_call(
        kernel,
        out_shape=outs,
        input_output_aliases=alias or {},
        compiler_params=pltpu.CompilerParams(vmem_limit_bytes=mib << 20),
        cost_estimate=pl.CostEstimate(flops=int(us * 1.1e9), bytes_accessed=0, transcendentals=0),
        **placed,
    )(place, *args)


def shape(*dims, dtype=BF16):
    return jax.ShapeDtypeStruct(dims, dtype)


def at(start, size, step=128):
    return pl.ds(pl.multiple_of(start, step), size)


def slot(place, k, j):
    return (place[3] + k) % 4 * 2 + (place[4] + j) % 2


def behind(place, axis, s):
    return (place[axis] + 4 + (2 * place[2] - 1) * s) % 4


def chunk_rows(place, s, rows):
    return at((4 + (2 * place[2] - 1) * s) % 4 * rows, rows, 128)


def pack_kernel(place, grad, weight, own, other, *parts):
    l, c = place[1], place[2]
    stripe = own.shape[1] // 8
    for out, side in ((own, l), (other, 1 - l)):
        for i, core in enumerate((c, 1 - c)):
            for k in range(4):
                to = pl.ds((i * 4 + k) * stripe, stripe)
                out[:, to] = grad[:, at((k * 4 + side * 2 + core) * stripe, stripe)]
    rows, columns = weight.shape[0], parts[0].shape[1]
    for k in range(4):
        parts[k][2 * rows :, :] = jnp.zeros_like(parts[k][2 * rows :, :])
    for n, (k, j) in enumerate(EIGHT):
        parts[k][j * rows : (j + 1) * rows, :] = weight[:, at(slot(place, k, j) * columns, columns)]


def split_kernel(place, *refs):
    parts, (keep, give) = refs[:4], refs[4:]
    rows, quarter = parts[0].shape[0], keep.shape[1]
    for n, part in enumerate(parts):
        keep[n * rows : (n + 1) * rows, :] = part[:, :quarter]
        give[n * rows : (n + 1) * rows, :] = part[:, quarter:]


def weight_kernel(place, *refs):
    parts, outs = refs[:4], refs[4:]
    rows = outs[0].shape[0] // 4
    for k, part in enumerate(parts):
        to = at((place[3] + k) % 4 * rows, rows, 32)
        for j, out in enumerate(outs):
            out[to, :] = part[j * rows : (j + 1) * rows, :]


def hidden_kernel(place, gate_ref, up_ref, out, gate_factor, up_factor):
    gate, up = gate_ref[...].astype(F32), up_ref[...].astype(F32)
    sig = jax.nn.sigmoid(gate)
    out[...] = (gate * sig * up).astype(BF16)
    gate_factor[...] = (up * sig * (1.0 + gate * (1.0 - sig))).astype(BF16)
    up_factor[...] = (gate * sig).astype(BF16)


def product_kernel(l, columns, count, place, *refs):
    chunks, weights, more, outs, (rows_of, all_of) = refs[:4], refs[4:12], refs[12 : -2 - count], refs[-2 - count : -2], refs[-2:]
    rows, cut = chunks[0].shape[0] // 2, weights[0].shape[0] // 4
    for s in range(4):
        rows_of[chunk_rows(place, s, rows), :] = chunks[s][l * rows : (l + 1) * rows, :]
        for j in range(2):
            for z in range(4):
                to = ((behind(place, 0, s) * 4 + z) * 2 + (place[4] + j) % 2) * cut
                all_of[at(to, cut, 32), :] = weights[4 * j + s][z * cut : (z + 1) * cut, columns]
    half = weights[0].shape[1] // 2
    for i in range(all_of.shape[1] // half):
        part = slice(i * half, (i + 1) * half)
        product = jnp.dot(rows_of[...], all_of[:, part], preferred_element_type=F32)
        if more:
            product = product + more[i][...].astype(F32)
        if count == 1:
            outs[0][:, part] = product.astype(outs[0].dtype)
        else:
            outs[i][...] = product.astype(outs[i].dtype)


def term_kernel(s, factor, place, *refs):
    chunks, rights, outs, lhs = refs[:8], refs[8:13], refs[13:15], refs[15]
    rows = chunks[0].shape[0] // 2
    cut, half = outs[0].shape
    block = at(behind(place, 0, s) * cut, cut, 256)
    for n, chunk in enumerate(chunks):
        to = chunk_rows(place, n % 4, rows)
        for l in range(2):
            lhs.at[pl.ds((2 * l + n // 4) * 4 * rows, 4 * rows), :][to, :] = chunk[l * rows : (l + 1) * rows, block]
    for i, out in enumerate(outs):
        product, start = None, 0
        for right in rights:
            left = lhs[start : start + right.shape[0], :]
            part = lax.dot_general(
                left, right[:, i * half : (i + 1) * half], (((0,), (0,)), ((), ())), preferred_element_type=F32
            )
            product, start = part if product is None else product + part, start + right.shape[0]
        out[...] = (product * factor).astype(BF16)


def chip_kernel(place, *refs):
    half, start = refs[0].shape[1], 0
    for out in refs[4:]:
        rows = slice(start, start + out.shape[0])
        for i in range(2):
            total = refs[i][rows, :] + refs[2 + i][rows, :].astype(F32)
            out[:, i * half : (i + 1) * half] = total.astype(BF16)
        start = rows.stop


def gradient_kernel(first, place, gate_factor, up_factor, mine, pair, *refs):
    outs, (stored, sem) = refs[-4:-2], refs[-2:]
    rows = mine.shape[0] // 8
    stores = []
    for n in range(pair.shape[0] // rows):
        here = slice((first + n) * rows, (first + n + 1) * rows)
        grad = mine[here, :] + pair[n * rows : (n + 1) * rows, :].astype(F32)
        block = at(slot(place, *EIGHT[first + n]) * rows, rows, 64)
        for i, (out, factor) in enumerate(zip(outs, (gate_factor, up_factor))):
            stored[n, i] = (grad * factor[here, :].astype(F32)).astype(BF16)
            stores.append(pltpu.make_async_copy(stored.at[n, i], out.at[block, :], sem.at[n, i]))
            stores[-1].start()
    for store in stores:
        store.wait()


def join_kernel(place, *refs):
    half = refs[0].shape[1]
    for i in range(2):
        total = refs[i][...].astype(F32) + refs[2 + i][...].astype(F32)
        refs[4][:, i * half : (i + 1) * half] = total.astype(BF16)


def tied(x, *first):
    return lax.optimization_barrier((x, first))[0]


def added(a, b):
    return (a.astype(F32) + b.astype(F32)).astype(BF16)


def on_device(gate_pre, up_pre, out_grad, down_weight):
    dp, tensor = lax.axis_index("dp"), lax.axis_index("tensor")
    place = jnp.stack([dp // 4, dp // 2 % 2, dp % 2, tensor // 2, tensor % 2]).astype(jnp.int32)
    tokens, columns = gate_pre.shape
    half = columns // 2
    share, width = out_grad.shape
    quarter = width // 4
    cut = quarter // 4
    shard = down_weight.shape[0]

    packed = call(
        pack_kernel, [shape(share, 2 * quarter)] * 2 + [shape(2 * shard + 16, columns)] * 4, place, out_grad, down_weight
    )
    o_own, o_other, parts = packed[0], packed[1], packed[2:]

    parts = [parts[0]] + [send(parts[4 - k], z=4 - k) for k in (1, 2, 3)]
    block = pl.BlockSpec((share, columns), lambda n, place: (slot(place, n // 2, n % 2), 0))
    there = pl.BlockSpec((share, columns), lambda n, place: (n, 0))
    hid_own, *factors = call(
        hidden_kernel, [shape(tokens, columns)] * 3, place, *tied((gate_pre, up_pre), o_own),
        specs=[block] * 2, grid=(8,), to=[there] * 3,
    )
    o_l, o_h, o_lh = send(o_other, l=1), send(tied(o_own, hid_own), h=1), send(o_other, l=1, h=1)
    near, give_h = call(weight_kernel, [shape(4 * shard, columns)] * 2, place, *tied(parts, hid_own))
    near, far = [near], [send(give_h, h=1)]
    own, give = call(split_kernel, [shape(4 * share, quarter)] * 2, place, *tied((o_own, o_h, o_l, o_lh), hid_own, near[0]))
    near.append(ring_y(near[0]))
    hid_pair = send(tied(hid_own, near[1], o_h, o_l, o_lh), l=1)
    own, core = [own], [send(give, c=1)]
    own.append(ring_z(own[0]))
    core.append(ring_z(core[0]))
    far.append(ring_y(far[0]))
    near.append(ring_y(near[1]))
    own.append(ring_z(own[1]))
    core.append(ring_z(core[1]))
    far.append(ring_y(far[1]))
    near.append(ring_y(near[2]))
    own.append(ring_z(own[2]))
    core.append(ring_z(core[2]))
    far.append(ring_y(far[2]))
    weights = near + far
    hid_core = [send(tied(x, far[3]), c=1) for x in (hid_own[: 2 * share], hid_own[2 * share :])]

    def hidden_grad(l, c, side, outs, *after, more=()):
        wide = slice(0, columns) if side is None else slice(side * half, (side + 1) * half)
        size = wide.stop - wide.start

        def kernel(*refs):
            product_kernel(l, wide, len(outs), *refs)

        return call(
            kernel, outs, place, *tied((own, core)[c], *after), *weights, *more,
            us=size / half * 1.6, scratch=[pltpu.VMEM((tokens, quarter), BF16), pltpu.VMEM((quarter, size), BF16)],
        )

    factor = 1.0 / float(np.sqrt(np.float32(tokens * 16)))

    def term(s, *after):
        def kernel(*refs):
            term_kernel(s, factor, *refs)

        return call(
            kernel, [shape(cut, half)] * 2, place, *tied(own + core, *after), hid_own, *hid_core, hid_pair, hid_last,
            us=3.1, scratch=[pltpu.VMEM((4 * tokens, cut), BF16)],
        )

    out = [shape(tokens, half)] * 2
    outs = hidden_grad(1, 1, None, out, hid_core[0])
    mine = hidden_grad(1, 0, None, [shape(tokens, half, dtype=F32)] * 2, outs[0])
    hid_last = send(tied(hid_pair, own[3], core[3], near[3], hid_core[0]), c=1)
    outs = [send(x, c=1) for x in outs]
    sizes = [6, 2]
    pairs = call(chip_kernel, [shape(n * share, columns) for n in sizes], place, *mine, *outs)
    first = term(1, mine[0])
    second = term(2, first[0])
    core_out = [send(x, c=1) for x in hidden_grad(0, 1, None, out, second[0])]
    first = [ring_y(x) for x in first]
    second = [ring_y(added(a, b)) for a, b in zip(second, first)]
    third = term(3, first[0])
    third_0 = third[0]
    (mine,) = hidden_grad(0, 0, None, [shape(tokens, columns, dtype=F32)], third[0], second[0], more=core_out)
    third = [ring_y(added(a, b)) for a, b in zip(third, second)]
    pairs = [send(x, l=1) for x in pairs]
    last = term(0, third_0)
    (down_grad,) = call(join_kernel, [shape(cut, columns)], place, *last, *third)

    def gradients(first, pair, mine, *before):
        def kernel(*refs):
            gradient_kernel(first, *refs)

        count = pair.shape[0] // share
        hbm = pl.BlockSpec(memory_space=pltpu.HBM)
        return call(
            kernel, [shape(tokens, columns)] * 2, place, *factors, mine, pair, *before,
            specs=[VMEM] * 4 + [hbm] * len(before), to=[hbm] * 2, alias={5 + i: i for i in range(len(before))},
            scratch=[pltpu.VMEM((count, 2, share, columns), BF16), pltpu.SemaphoreType.DMA((count, 2))],
        )

    gradient = gradients(0, pairs[0], mine)
    gate_grad, up_grad = gradients(sizes[0], pairs[1], tied(mine, down_grad), *gradient)
    return (gate_grad, up_grad, down_grad)


def solution(mesh):
    return jax.shard_map(
        on_device,
        mesh=mesh,
        in_specs=(
            P("dp", "tensor"),
            P("dp", "tensor"),
            P(("dp", "tensor"), None),
            P(("dp", "tensor"), None),
        ),
        out_specs=(P("dp", "tensor"), P("dp", "tensor"), P("dp", "tensor")),
        check_vma=False,
    )
```

```python
import jax
import jax.numpy as jnp
import numpy as np
from jax import lax
from jax.experimental import pallas as pl
from jax.experimental.pallas import tpu as pltpu
from jax.sharding import PartitionSpec as P

SIZES = (4, 2, 2, 4, 2)
BF16, F32 = jnp.bfloat16, jnp.float32
VMEM = pl.BlockSpec(memory_space=pltpu.VMEM)
SMEM = pl.BlockSpec(memory_space=pltpu.SMEM)
EIGHT = [(k, j) for k in range(4) for j in range(2)]


def permuted(x, step):
    pairs = []
    for source in range(int(np.prod(SIZES))):
        place = [int(p) for p in np.unravel_index(source, SIZES)]
        target = [(p + d) % n for p, d, n in zip(place, step(place[2]), SIZES)]
        pairs.append((source, int(np.ravel_multi_index(target, SIZES))))
    return lax.ppermute(x, ("dp", "tensor"), pairs)


def send(x, y=0, l=0, c=0, z=0, h=0):
    return permuted(x, lambda core: (y, l, c, z, h))


def ring_y(x):
    return permuted(x, lambda core: (1 - 2 * core, 0, 0, 0, 0))


def ring_z(x):
    return permuted(x, lambda core: (0, 0, 0, 1 - 2 * core, 0))


def call(kernel, outs, place, *args, mib=24, specs=None, grid=None, to=None, scratch=(), us=0.0, alias=None):
    specs, to = specs or [VMEM] * len(args), to or [VMEM] * len(outs)
    if grid is None:
        placed = dict(in_specs=[SMEM] + specs, out_specs=to, scratch_shapes=scratch)
    else:
        placed = dict(
            grid_spec=pltpu.PrefetchScalarGridSpec(
                num_scalar_prefetch=1, grid=grid, in_specs=specs, out_specs=to, scratch_shapes=scratch
            )
        )
    return pl.pallas_call(
        kernel,
        out_shape=outs,
        input_output_aliases=alias or {},
        compiler_params=pltpu.CompilerParams(vmem_limit_bytes=mib << 20),
        cost_estimate=pl.CostEstimate(flops=int(us * 1.1e9), bytes_accessed=0, transcendentals=0),
        **placed,
    )(place, *args)


def shape(*dims, dtype=BF16):
    return jax.ShapeDtypeStruct(dims, dtype)


def at(start, size, step=128):
    return pl.ds(pl.multiple_of(start, step), size)


def slot(place, k, j):
    return (place[3] + k) % 4 * 2 + (place[4] + j) % 2


def behind(place, axis, s):
    return (place[axis] + 4 + (2 * place[2] - 1) * s) % 4


def chunk_rows(place, s, rows):
    return at((4 + (2 * place[2] - 1) * s) % 4 * rows, rows, 128)


def pack_kernel(place, grad, weight, own, other, *parts):
    l, c = place[1], place[2]
    stripe = own.shape[1] // 8
    for out, side in ((own, l), (other, 1 - l)):
        for i, core in enumerate((c, 1 - c)):
            for k in range(4):
                to = pl.ds((i * 4 + k) * stripe, stripe)
                out[:, to] = grad[:, at((k * 4 + side * 2 + core) * stripe, stripe)]
    rows, columns = weight.shape[0], parts[0].shape[1]
    for n, (k, j) in enumerate(EIGHT):
        parts[k][j * rows : (j + 1) * rows, :] = weight[:, at(slot(place, k, j) * columns, columns)]


def split_kernel(place, *refs):
    parts, (keep, give) = refs[:4], refs[4:]
    rows, quarter = parts[0].shape[0], keep.shape[1]
    for n, part in enumerate(parts):
        keep[n * rows : (n + 1) * rows, :] = part[:, :quarter]
        give[n * rows : (n + 1) * rows, :] = part[:, quarter:]


def weight_kernel(place, *refs):
    parts, outs = refs[:4], refs[4:]
    rows = outs[0].shape[0] // 4
    for k, part in enumerate(parts):
        to = at((place[3] + k) % 4 * rows, rows, 32)
        for j, out in enumerate(outs):
            out[to, :] = part[j * rows : (j + 1) * rows, :]


def hidden_kernel(place, gate_ref, up_ref, out, gate_factor, up_factor):
    gate, up = gate_ref[...].astype(F32), up_ref[...].astype(F32)
    sig = jax.nn.sigmoid(gate)
    out[...] = (gate * sig * up).astype(BF16)
    gate_factor[...] = (up * sig * (1.0 + gate * (1.0 - sig))).astype(BF16)
    up_factor[...] = (gate * sig).astype(BF16)


def product_kernel(l, columns, count, place, *refs):
    chunks, weights, more, outs, (rows_of, all_of) = refs[:4], refs[4:12], refs[12 : -2 - count], refs[-2 - count : -2], refs[-2:]
    rows, cut = chunks[0].shape[0] // 2, weights[0].shape[0] // 4
    for s in range(4):
        rows_of[chunk_rows(place, s, rows), :] = chunks[s][l * rows : (l + 1) * rows, :]
        for j in range(2):
            for z in range(4):
                to = ((behind(place, 0, s) * 4 + z) * 2 + (place[4] + j) % 2) * cut
                all_of[at(to, cut, 32), :] = weights[4 * j + s][z * cut : (z + 1) * cut, columns]
    half = weights[0].shape[1] // 2
    for i in range(all_of.shape[1] // half):
        part = slice(i * half, (i + 1) * half)
        product = jnp.dot(rows_of[...], all_of[:, part], preferred_element_type=F32)
        if more:
            product = product + more[i][...].astype(F32)
        if count == 1:
            outs[0][:, part] = product.astype(outs[0].dtype)
        else:
            outs[i][...] = product.astype(outs[i].dtype)


def term_kernel(s, factor, place, *refs):
    chunks, rights, outs, lhs = refs[:8], refs[8:13], refs[13:15], refs[15]
    rows = chunks[0].shape[0] // 2
    cut, half = outs[0].shape
    block = at(behind(place, 0, s) * cut, cut, 256)
    for n, chunk in enumerate(chunks):
        to = chunk_rows(place, n % 4, rows)
        for l in range(2):
            lhs.at[pl.ds((2 * l + n // 4) * 4 * rows, 4 * rows), :][to, :] = chunk[l * rows : (l + 1) * rows, block]
    for i, out in enumerate(outs):
        product, start = None, 0
        for right in rights:
            left = lhs[start : start + right.shape[0], :]
            part = lax.dot_general(
                left, right[:, i * half : (i + 1) * half], (((0,), (0,)), ((), ())), preferred_element_type=F32
            )
            product, start = part if product is None else product + part, start + right.shape[0]
        out[...] = (product * factor).astype(BF16)


def chip_kernel(place, *refs):
    half, start = refs[0].shape[1], 0
    for out in refs[4:]:
        rows = slice(start, start + out.shape[0])
        for i in range(2):
            total = refs[i][rows, :] + refs[2 + i][rows, :].astype(F32)
            out[:, i * half : (i + 1) * half] = total.astype(BF16)
        start = rows.stop


def gradient_kernel(first, place, gate_factor, up_factor, mine, pair, *refs):
    outs, (stored, sem) = refs[-4:-2], refs[-2:]
    rows = mine.shape[0] // 8
    stores = []
    for n in range(pair.shape[0] // rows):
        here = slice((first + n) * rows, (first + n + 1) * rows)
        grad = mine[here, :] + pair[n * rows : (n + 1) * rows, :].astype(F32)
        block = at(slot(place, *EIGHT[first + n]) * rows, rows, 64)
        for i, (out, factor) in enumerate(zip(outs, (gate_factor, up_factor))):
            stored[n, i] = (grad * factor[here, :].astype(F32)).astype(BF16)
            stores.append(pltpu.make_async_copy(stored.at[n, i], out.at[block, :], sem.at[n, i]))
            stores[-1].start()
    for store in stores:
        store.wait()


def join_kernel(place, *refs):
    half = refs[0].shape[1]
    for i in range(2):
        total = refs[i][...].astype(F32) + refs[2 + i][...].astype(F32)
        refs[4][:, i * half : (i + 1) * half] = total.astype(BF16)


def tied(x, *first):
    return lax.optimization_barrier((x, first))[0]


def added(a, b):
    return (a.astype(F32) + b.astype(F32)).astype(BF16)


def on_device(gate_pre, up_pre, out_grad, down_weight):
    dp, tensor = lax.axis_index("dp"), lax.axis_index("tensor")
    place = jnp.stack([dp // 4, dp // 2 % 2, dp % 2, tensor // 2, tensor % 2]).astype(jnp.int32)
    tokens, columns = gate_pre.shape
    half = columns // 2
    share, width = out_grad.shape
    quarter = width // 4
    cut = quarter // 4
    shard = down_weight.shape[0]

    packed = call(
        pack_kernel, [shape(share, 2 * quarter)] * 2 + [shape(2 * shard, columns)] * 4, place, out_grad, down_weight
    )
    o_own, o_other, parts = packed[0], packed[1], packed[2:]

    parts = [parts[0]] + [send(parts[4 - k], z=4 - k) for k in (1, 2, 3)]
    block = pl.BlockSpec((share, columns), lambda n, place: (slot(place, n // 2, n % 2), 0))
    there = pl.BlockSpec((share, columns), lambda n, place: (n, 0))
    hid_own, *factors = call(
        hidden_kernel, [shape(tokens, columns)] * 3, place, *tied((gate_pre, up_pre), o_own),
        specs=[block] * 2, grid=(8,), to=[there] * 3,
    )
    o_l, o_h, o_lh = send(tied(o_other, hid_own), l=1), send(o_own, h=1), send(o_other, l=1, h=1)
    near, give_h = call(weight_kernel, [shape(4 * shard, columns)] * 2, place, *tied(parts, hid_own))
    near, far = [near], [send(give_h, h=1)]
    own, give = call(split_kernel, [shape(4 * share, quarter)] * 2, place, *tied((o_own, o_h, o_l, o_lh), hid_own, near[0]))
    near.append(ring_y(near[0]))
    hid_pair = send(tied(hid_own, near[1], o_h, o_l, o_lh), l=1)
    own, core = [own], [send(give, c=1)]
    own.append(ring_z(own[0]))
    core.append(ring_z(core[0]))
    far.append(ring_y(far[0]))
    near.append(ring_y(near[1]))
    own.append(ring_z(own[1]))
    core.append(ring_z(core[1]))
    far.append(ring_y(far[1]))
    near.append(ring_y(near[2]))
    own.append(ring_z(own[2]))
    core.append(ring_z(core[2]))
    far.append(ring_y(far[2]))
    weights = near + far
    hid_core = [send(tied(x, far[3]), c=1) for x in (hid_own[: 2 * share], hid_own[2 * share :])]

    def hidden_grad(l, c, side, outs, *after, more=()):
        wide = slice(0, columns) if side is None else slice(side * half, (side + 1) * half)
        size = wide.stop - wide.start

        def kernel(*refs):
            product_kernel(l, wide, len(outs), *refs)

        return call(
            kernel, outs, place, *tied((own, core)[c], *after), *weights, *more,
            us=size / half * 1.6, scratch=[pltpu.VMEM((tokens, quarter), BF16), pltpu.VMEM((quarter, size), BF16)],
        )

    factor = 1.0 / float(np.sqrt(np.float32(tokens * 16)))

    def term(s, *after):
        def kernel(*refs):
            term_kernel(s, factor, *refs)

        return call(
            kernel, [shape(cut, half)] * 2, place, *tied(own + core, *after), hid_own, *hid_core, hid_pair, hid_last,
            us=3.1, scratch=[pltpu.VMEM((4 * tokens, cut), BF16)],
        )

    out = [shape(tokens, half)] * 2
    outs = hidden_grad(1, 1, None, out, hid_core[0])
    mine = hidden_grad(1, 0, None, [shape(tokens, half, dtype=F32)] * 2, outs[0])
    hid_last = send(tied(hid_pair, own[3], core[3], near[3], hid_core[0]), c=1)
    outs = [send(x, c=1) for x in outs]
    sizes = [6, 2]
    pairs = call(chip_kernel, [shape(n * share, columns) for n in sizes], place, *mine, *outs)
    first = term(1, mine[0])
    second = term(2, first[0])
    core_out = [send(x, c=1) for x in hidden_grad(0, 1, None, out, second[0])]
    first = [ring_y(x) for x in first]
    second = [ring_y(added(a, b)) for a, b in zip(second, first)]
    third = term(3, first[0])
    third_0 = third[0]
    (mine,) = hidden_grad(0, 0, None, [shape(tokens, columns, dtype=F32)], third[0], second[0], more=core_out)
    third = [ring_y(added(a, b)) for a, b in zip(third, second)]
    pairs = [send(x, l=1) for x in pairs]
    last = term(0, third_0)
    (down_grad,) = call(join_kernel, [shape(cut, columns)], place, *last, *third)

    def gradients(first, pair, mine, *before):
        def kernel(*refs):
            gradient_kernel(first, *refs)

        count = pair.shape[0] // share
        hbm = pl.BlockSpec(memory_space=pltpu.HBM)
        return call(
            kernel, [shape(tokens, columns)] * 2, place, *factors, mine, pair, *before,
            specs=[VMEM] * 4 + [hbm] * len(before), to=[hbm] * 2, alias={5 + i: i for i in range(len(before))},
            scratch=[pltpu.VMEM((count, 2, share, columns), BF16), pltpu.SemaphoreType.DMA((count, 2))],
        )

    gradient = gradients(0, pairs[0], mine)
    gate_grad, up_grad = gradients(sizes[0], pairs[1], tied(mine, down_grad), *gradient)
    return (gate_grad, up_grad, down_grad)


def solution(mesh):
    return jax.shard_map(
        on_device,
        mesh=mesh,
        in_specs=(
            P("dp", "tensor"),
            P("dp", "tensor"),
            P(("dp", "tensor"), None),
            P(("dp", "tensor"), None),
        ),
        out_specs=(P("dp", "tensor"), P("dp", "tensor"), P("dp", "tensor")),
        check_vma=False,
    )
```

```python
import jax
import jax.numpy as jnp
import numpy as np
from jax import lax
from jax.experimental import pallas as pl
from jax.experimental.pallas import tpu as pltpu
from jax.sharding import PartitionSpec as P

SIZES = (4, 2, 2, 4, 2)
BF16, F32 = jnp.bfloat16, jnp.float32
VMEM = pl.BlockSpec(memory_space=pltpu.VMEM)
SMEM = pl.BlockSpec(memory_space=pltpu.SMEM)
EIGHT = [(k, j) for k in range(4) for j in range(2)]


def permuted(x, step):
    pairs = []
    for source in range(int(np.prod(SIZES))):
        place = [int(p) for p in np.unravel_index(source, SIZES)]
        target = [(p + d) % n for p, d, n in zip(place, step(place[2]), SIZES)]
        pairs.append((source, int(np.ravel_multi_index(target, SIZES))))
    return lax.ppermute(x, ("dp", "tensor"), pairs)


def send(x, y=0, l=0, c=0, z=0, h=0):
    return permuted(x, lambda core: (y, l, c, z, h))


def ring_y(x):
    return permuted(x, lambda core: (1 - 2 * core, 0, 0, 0, 0))


def ring_z(x):
    return permuted(x, lambda core: (0, 0, 0, 1 - 2 * core, 0))


def call(kernel, outs, place, *args, mib=24, specs=None, grid=None, to=None, scratch=(), us=0.0, alias=None):
    specs, to = specs or [VMEM] * len(args), to or [VMEM] * len(outs)
    if grid is None:
        placed = dict(in_specs=[SMEM] + specs, out_specs=to, scratch_shapes=scratch)
    else:
        placed = dict(
            grid_spec=pltpu.PrefetchScalarGridSpec(
                num_scalar_prefetch=1, grid=grid, in_specs=specs, out_specs=to, scratch_shapes=scratch
            )
        )
    return pl.pallas_call(
        kernel,
        out_shape=outs,
        input_output_aliases=alias or {},
        compiler_params=pltpu.CompilerParams(vmem_limit_bytes=mib << 20),
        cost_estimate=pl.CostEstimate(flops=int(us * 1.1e9), bytes_accessed=0, transcendentals=0),
        **placed,
    )(place, *args)


def shape(*dims, dtype=BF16):
    return jax.ShapeDtypeStruct(dims, dtype)


def at(start, size, step=128):
    return pl.ds(pl.multiple_of(start, step), size)


def slot(place, k, j):
    return (place[3] + k) % 4 * 2 + (place[4] + j) % 2


def behind(place, axis, s):
    return (place[axis] + 4 + (2 * place[2] - 1) * s) % 4


def chunk_rows(place, s, rows):
    return at((4 + (2 * place[2] - 1) * s) % 4 * rows, rows, 128)


def pack_kernel(place, grad, weight, own, other, *parts):
    l, c = place[1], place[2]
    stripe = own.shape[1] // 8
    for out, side in ((own, l), (other, 1 - l)):
        for i, core in enumerate((c, 1 - c)):
            for k in range(4):
                to = pl.ds((i * 4 + k) * stripe, stripe)
                out[:, to] = grad[:, at((k * 4 + side * 2 + core) * stripe, stripe)]
    rows, columns = weight.shape[0], parts[0].shape[1]
    for n, (k, j) in enumerate(EIGHT):
        parts[k][j * rows : (j + 1) * rows, :] = weight[:, at(slot(place, k, j) * columns, columns)]


def split_kernel(place, *refs):
    parts, (keep, give) = refs[:4], refs[4:]
    rows, quarter = parts[0].shape[0], keep.shape[1]
    for n, part in enumerate(parts):
        keep[n * rows : (n + 1) * rows, :] = part[:, :quarter]
        give[n * rows : (n + 1) * rows, :] = part[:, quarter:]


def weight_kernel(place, *refs):
    parts, outs = refs[:4], refs[4:]
    rows = outs[0].shape[0] // 4
    for k, part in enumerate(parts):
        to = at((place[3] + k) % 4 * rows, rows, 32)
        for j, out in enumerate(outs):
            out[to, :] = part[j * rows : (j + 1) * rows, :]


def hidden_kernel(place, gate_ref, up_ref, out, gate_factor, up_factor):
    gate, up = gate_ref[...].astype(F32), up_ref[...].astype(F32)
    sig = jax.nn.sigmoid(gate)
    out[...] = (gate * sig * up).astype(BF16)
    gate_factor[...] = (up * sig * (1.0 + gate * (1.0 - sig))).astype(BF16)
    up_factor[...] = (gate * sig).astype(BF16)


def product_kernel(l, columns, count, place, *refs):
    chunks, weights, more, outs, (rows_of, all_of) = refs[:4], refs[4:12], refs[12 : -2 - count], refs[-2 - count : -2], refs[-2:]
    rows, cut = chunks[0].shape[0] // 2, weights[0].shape[0] // 4
    for s in range(4):
        rows_of[chunk_rows(place, s, rows), :] = chunks[s][l * rows : (l + 1) * rows, :]
        for j in range(2):
            for z in range(4):
                to = ((behind(place, 0, s) * 4 + z) * 2 + (place[4] + j) % 2) * cut
                all_of[at(to, cut, 32), :] = weights[4 * j + s][z * cut : (z + 1) * cut, columns]
    half = weights[0].shape[1] // 2
    for i in range(all_of.shape[1] // half):
        part = slice(i * half, (i + 1) * half)
        product = jnp.dot(rows_of[...], all_of[:, part], preferred_element_type=F32)
        if more:
            product = product + more[i][...].astype(F32)
        if count == 1:
            outs[0][:, part] = product.astype(outs[0].dtype)
        else:
            outs[i][...] = product.astype(outs[i].dtype)


def term_kernel(s, factor, place, *refs):
    chunks, rights, outs, lhs = refs[:8], refs[8:13], refs[13:15], refs[15]
    rows = chunks[0].shape[0] // 2
    cut, half = outs[0].shape
    block = at(behind(place, 0, s) * cut, cut, 256)
    for n, chunk in enumerate(chunks):
        to = chunk_rows(place, n % 4, rows)
        for l in range(2):
            lhs.at[pl.ds((2 * l + n // 4) * 4 * rows, 4 * rows), :][to, :] = chunk[l * rows : (l + 1) * rows, block]
    for i, out in enumerate(outs):
        product, start = None, 0
        for right in rights:
            left = lhs[start : start + right.shape[0], :]
            part = lax.dot_general(
                left, right[:, i * half : (i + 1) * half], (((0,), (0,)), ((), ())), preferred_element_type=F32
            )
            product, start = part if product is None else product + part, start + right.shape[0]
        out[...] = (product * factor).astype(BF16)


def chip_kernel(place, mine, core, *outs):
    start = 0
    for out in outs:
        rows = slice(start, start + out.shape[0])
        out[...] = (mine[rows, :] + core[rows, :].astype(F32)).astype(BF16)
        start = rows.stop


def gradient_kernel(first, place, gate_factor, up_factor, mine, pair, *refs):
    outs, (stored, sem) = refs[-4:-2], refs[-2:]
    rows = mine.shape[0] // 8
    stores = []
    for n in range(pair.shape[0] // rows):
        here = slice((first + n) * rows, (first + n + 1) * rows)
        grad = mine[here, :] + pair[n * rows : (n + 1) * rows, :].astype(F32)
        block = at(slot(place, *EIGHT[first + n]) * rows, rows, 64)
        for i, (out, factor) in enumerate(zip(outs, (gate_factor, up_factor))):
            stored[n, i] = (grad * factor[here, :].astype(F32)).astype(BF16)
            stores.append(pltpu.make_async_copy(stored.at[n, i], out.at[block, :], sem.at[n, i]))
            stores[-1].start()
    for store in stores:
        store.wait()


def join_kernel(place, *refs):
    half = refs[0].shape[1]
    for i in range(2):
        total = refs[i][...].astype(F32) + refs[2 + i][...].astype(F32)
        refs[4][:, i * half : (i + 1) * half] = total.astype(BF16)


def tied(x, *first):
    return lax.optimization_barrier((x, first))[0]


def added(a, b):
    return (a.astype(F32) + b.astype(F32)).astype(BF16)


def on_device(gate_pre, up_pre, out_grad, down_weight):
    dp, tensor = lax.axis_index("dp"), lax.axis_index("tensor")
    place = jnp.stack([dp // 4, dp // 2 % 2, dp % 2, tensor // 2, tensor % 2]).astype(jnp.int32)
    tokens, columns = gate_pre.shape
    half = columns // 2
    share, width = out_grad.shape
    quarter = width // 4
    cut = quarter // 4
    shard = down_weight.shape[0]

    packed = call(
        pack_kernel, [shape(share, 2 * quarter)] * 2 + [shape(2 * shard, columns)] * 4, place, out_grad, down_weight
    )
    o_own, o_other, parts = packed[0], packed[1], packed[2:]

    parts = [parts[0]] + [send(parts[4 - k], z=4 - k) for k in (1, 2, 3)]
    block = pl.BlockSpec((share, columns), lambda n, place: (slot(place, n // 2, n % 2), 0))
    there = pl.BlockSpec((share, columns), lambda n, place: (n, 0))
    hid_own, *factors = call(
        hidden_kernel, [shape(tokens, columns)] * 3, place, *tied((gate_pre, up_pre), o_own),
        specs=[block] * 2, grid=(8,), to=[there] * 3,
    )
    o_l, o_h, o_lh = send(tied(o_other, hid_own), l=1), send(o_own, h=1), send(o_other, l=1, h=1)
    near, give_h = call(weight_kernel, [shape(4 * shard, columns)] * 2, place, *tied(parts, hid_own))
    near, far = [near], [send(give_h, h=1)]
    own, give = call(split_kernel, [shape(4 * share, quarter)] * 2, place, *tied((o_own, o_h, o_l, o_lh), hid_own, near[0]))
    near.append(ring_y(near[0]))
    hid_pair = send(tied(hid_own, near[1], o_h, o_l, o_lh), l=1)
    own, core = [own], [send(give, c=1)]
    own.append(ring_z(own[0]))
    core.append(ring_z(core[0]))
    far.append(ring_y(far[0]))
    near.append(ring_y(near[1]))
    own.append(ring_z(own[1]))
    core.append(ring_z(core[1]))
    far.append(ring_y(far[1]))
    near.append(ring_y(near[2]))
    own.append(ring_z(own[2]))
    core.append(ring_z(core[2]))
    far.append(ring_y(far[2]))
    weights = near + far
    hid_core = [send(tied(hid_own[: 2 * share], far[3], near[3]), c=1), send(tied(hid_own[2 * share :], far[3]), c=1)]

    def hidden_grad(l, c, side, outs, *after, more=()):
        wide = slice(0, columns) if side is None else slice(side * half, (side + 1) * half)
        size = wide.stop - wide.start

        def kernel(*refs):
            product_kernel(l, wide, len(outs), *refs)

        return call(
            kernel, outs, place, *tied((own, core)[c], *after), *weights, *more,
            us=0.0 if l else 3.2, scratch=[pltpu.VMEM((tokens, quarter), BF16), pltpu.VMEM((quarter, size), BF16)],
        )

    factor = 1.0 / float(np.sqrt(np.float32(tokens * 16)))

    def term(s, *after):
        def kernel(*refs):
            term_kernel(s, factor, *refs)

        return call(
            kernel, [shape(cut, half)] * 2, place, *tied(own + core, *after), hid_own, *hid_core, hid_pair, hid_last,
            us=3.1, scratch=[pltpu.VMEM((4 * tokens, cut), BF16)],
        )

    out = [shape(tokens, half)] * 2
    (chip_out,) = hidden_grad(1, 1, None, [shape(tokens, columns)], hid_core[0])
    (mine,) = hidden_grad(1, 0, None, [shape(tokens, columns, dtype=F32)], chip_out)
    chip_out = send(chip_out, c=1)
    hid_last = send(tied(hid_pair, mine, hid_core[0]), c=1)
    sizes = [8]
    pairs = call(chip_kernel, [shape(n * share, columns) for n in sizes], place, mine, chip_out)
    first = term(1, pairs[0])
    second = term(2, first[0])
    core_out = [send(x, c=1) for x in hidden_grad(0, 1, None, out, second[0])]
    first = [ring_y(x) for x in first]
    second = [ring_y(added(a, b)) for a, b in zip(second, first)]
    third = term(3, first[0])
    third_0 = third[0]
    (mine,) = hidden_grad(0, 0, None, [shape(tokens, columns, dtype=F32)], third[0], second[0], more=core_out)
    third = [ring_y(added(a, b)) for a, b in zip(third, second)]
    pairs = [send(x, l=1) for x in pairs]
    last = term(0, third_0)
    (down_grad,) = call(join_kernel, [shape(cut, columns)], place, *last, *third)

    def gradients(first, pair, mine, *before):
        def kernel(*refs):
            gradient_kernel(first, *refs)

        count = pair.shape[0] // share
        hbm = pl.BlockSpec(memory_space=pltpu.HBM)
        return call(
            kernel, [shape(tokens, columns)] * 2, place, *factors, mine, pair, *before,
            specs=[VMEM] * 4 + [hbm] * len(before), to=[hbm] * 2, alias={5 + i: i for i in range(len(before))},
            scratch=[pltpu.VMEM((count, 2, share, columns), BF16), pltpu.SemaphoreType.DMA((count, 2))],
        )

    gate_grad, up_grad = gradients(0, pairs[0], tied(mine, down_grad))
    return (gate_grad, up_grad, down_grad)


def solution(mesh):
    return jax.shard_map(
        on_device,
        mesh=mesh,
        in_specs=(
            P("dp", "tensor"),
            P("dp", "tensor"),
            P(("dp", "tensor"), None),
            P(("dp", "tensor"), None),
        ),
        out_specs=(P("dp", "tensor"), P("dp", "tensor"), P("dp", "tensor")),
        check_vma=False,
    )
```

```python
import jax
import jax.numpy as jnp
import numpy as np
from jax import lax
from jax.experimental import pallas as pl
from jax.experimental.pallas import tpu as pltpu
from jax.sharding import PartitionSpec as P

SIZES = (4, 2, 2, 4, 2)
BF16, F32 = jnp.bfloat16, jnp.float32
VMEM = pl.BlockSpec(memory_space=pltpu.VMEM)
SMEM = pl.BlockSpec(memory_space=pltpu.SMEM)
EIGHT = [(k, j) for k in range(4) for j in range(2)]


def permuted(x, step):
    pairs = []
    for source in range(int(np.prod(SIZES))):
        place = [int(p) for p in np.unravel_index(source, SIZES)]
        target = [(p + d) % n for p, d, n in zip(place, step(place[2]), SIZES)]
        pairs.append((source, int(np.ravel_multi_index(target, SIZES))))
    return lax.ppermute(x, ("dp", "tensor"), pairs)


def send(x, y=0, l=0, c=0, z=0, h=0):
    return permuted(x, lambda core: (y, l, c, z, h))


def ring_y(x):
    return permuted(x, lambda core: (1 - 2 * core, 0, 0, 0, 0))


def ring_z(x):
    return permuted(x, lambda core: (0, 0, 0, 1 - 2 * core, 0))


def call(kernel, outs, place, *args, mib=24, specs=None, grid=None, to=None, scratch=(), us=0.0, alias=None):
    specs, to = specs or [VMEM] * len(args), to or [VMEM] * len(outs)
    if grid is None:
        placed = dict(in_specs=[SMEM] + specs, out_specs=to, scratch_shapes=scratch)
    else:
        placed = dict(
            grid_spec=pltpu.PrefetchScalarGridSpec(
                num_scalar_prefetch=1, grid=grid, in_specs=specs, out_specs=to, scratch_shapes=scratch
            )
        )
    return pl.pallas_call(
        kernel,
        out_shape=outs,
        input_output_aliases=alias or {},
        compiler_params=pltpu.CompilerParams(vmem_limit_bytes=mib << 20),
        cost_estimate=pl.CostEstimate(flops=int(us * 1.1e9), bytes_accessed=0, transcendentals=0),
        **placed,
    )(place, *args)


def shape(*dims, dtype=BF16):
    return jax.ShapeDtypeStruct(dims, dtype)


def at(start, size, step=128):
    return pl.ds(pl.multiple_of(start, step), size)


def slot(place, k, j):
    return (place[3] + k) % 4 * 2 + (place[4] + j) % 2


def behind(place, axis, s):
    return (place[axis] + 4 + (2 * place[2] - 1) * s) % 4


def chunk_rows(place, s, rows):
    return at((4 + (2 * place[2] - 1) * s) % 4 * rows, rows, 128)


def pack_kernel(place, grad, weight, own, other, *parts):
    l, c = place[1], place[2]
    stripe = own.shape[1] // 8
    for out, side in ((own, l), (other, 1 - l)):
        for i, core in enumerate((c, 1 - c)):
            for k in range(4):
                to = pl.ds((i * 4 + k) * stripe, stripe)
                out[:, to] = grad[:, at((k * 4 + side * 2 + core) * stripe, stripe)]
    rows, columns = weight.shape[0], parts[0].shape[1]
    for n, (k, j) in enumerate(EIGHT):
        parts[k][j * rows : (j + 1) * rows, :] = weight[:, at(slot(place, k, j) * columns, columns)]


def split_kernel(place, *refs):
    parts, (keep, give) = refs[:4], refs[4:]
    rows, quarter = parts[0].shape[0], keep.shape[1]
    for n, part in enumerate(parts):
        keep[n * rows : (n + 1) * rows, :] = part[:, :quarter]
        give[n * rows : (n + 1) * rows, :] = part[:, quarter:]


def weight_kernel(place, *refs):
    parts, outs = refs[:4], refs[4:]
    rows = outs[0].shape[0] // 4
    for k, part in enumerate(parts):
        to = at((place[3] + k) % 4 * rows, rows, 32)
        for j, out in enumerate(outs):
            out[to, :] = part[j * rows : (j + 1) * rows, :]


def hidden_kernel(place, gate_ref, up_ref, out, gate_factor, up_factor):
    gate, up = gate_ref[...].astype(F32), up_ref[...].astype(F32)
    sig = jax.nn.sigmoid(gate)
    out[...] = (gate * sig * up).astype(BF16)
    gate_factor[...] = (up * sig * (1.0 + gate * (1.0 - sig))).astype(BF16)
    up_factor[...] = (gate * sig).astype(BF16)


def rows_kernel(place, *refs):
    weights, out = refs[:8], refs[8]
    cut = weights[0].shape[0] // 4
    for s in range(4):
        for j in range(2):
            for z in range(4):
                to = ((behind(place, 0, s) * 4 + z) * 2 + (place[4] + j) % 2) * cut
                out[at(to, cut, 32), :] = weights[4 * j + s][z * cut : (z + 1) * cut, :]


def product_kernel(l, count, place, *refs):
    chunks, weight, more, outs, rows_of = refs[:4], refs[4], refs[5 : -1 - count], refs[-1 - count : -1], refs[-1]
    rows = chunks[0].shape[0] // 2
    for s in range(4):
        rows_of[chunk_rows(place, s, rows), :] = chunks[s][l * rows : (l + 1) * rows, :]
    half = weight.shape[1] // 2
    for i in range(2):
        part = slice(i * half, (i + 1) * half)
        product = jnp.dot(rows_of[...], weight[:, part], preferred_element_type=F32)
        if more:
            product = product + more[i][...].astype(F32)
        if count == 1:
            outs[0][:, part] = product.astype(outs[0].dtype)
        else:
            outs[i][...] = product.astype(outs[i].dtype)


def term_kernel(s, factor, place, *refs):
    chunks, rights, outs, lhs = refs[:8], refs[8:13], refs[13:15], refs[15]
    rows = chunks[0].shape[0] // 2
    cut, half = outs[0].shape
    block = at(behind(place, 0, s) * cut, cut, 256)
    for n, chunk in enumerate(chunks):
        to = chunk_rows(place, n % 4, rows)
        for l in range(2):
            lhs.at[pl.ds((2 * l + n // 4) * 4 * rows, 4 * rows), :][to, :] = chunk[l * rows : (l + 1) * rows, block]
    for i, out in enumerate(outs):
        product, start = None, 0
        for right in rights:
            left = lhs[start : start + right.shape[0], :]
            part = lax.dot_general(
                left, right[:, i * half : (i + 1) * half], (((0,), (0,)), ((), ())), preferred_element_type=F32
            )
            product, start = part if product is None else product + part, start + right.shape[0]
        out[...] = (product * factor).astype(BF16)


def chip_kernel(place, mine, core, *outs):
    start = 0
    for out in outs:
        rows = slice(start, start + out.shape[0])
        out[...] = (mine[rows, :] + core[rows, :].astype(F32)).astype(BF16)
        start = rows.stop


def gradient_kernel(first, place, gate_factor, up_factor, mine, pair, *refs):
    outs, (stored, sem) = refs[-4:-2], refs[-2:]
    rows = mine.shape[0] // 8
    stores = []
    for n in range(pair.shape[0] // rows):
        here = slice((first + n) * rows, (first + n + 1) * rows)
        grad = mine[here, :] + pair[n * rows : (n + 1) * rows, :].astype(F32)
        block = at(slot(place, *EIGHT[first + n]) * rows, rows, 64)
        for i, (out, factor) in enumerate(zip(outs, (gate_factor, up_factor))):
            stored[n, i] = (grad * factor[here, :].astype(F32)).astype(BF16)
            stores.append(pltpu.make_async_copy(stored.at[n, i], out.at[block, :], sem.at[n, i]))
            stores[-1].start()
    for store in stores:
        store.wait()


def join_kernel(place, *refs):
    half = refs[0].shape[1]
    for i in range(2):
        total = refs[i][...].astype(F32) + refs[2 + i][...].astype(F32)
        refs[4][:, i * half : (i + 1) * half] = total.astype(BF16)


def tied(x, *first):
    return lax.optimization_barrier((x, first))[0]


def added(a, b):
    return (a.astype(F32) + b.astype(F32)).astype(BF16)


def on_device(gate_pre, up_pre, out_grad, down_weight):
    dp, tensor = lax.axis_index("dp"), lax.axis_index("tensor")
    place = jnp.stack([dp // 4, dp // 2 % 2, dp % 2, tensor // 2, tensor % 2]).astype(jnp.int32)
    tokens, columns = gate_pre.shape
    half = columns // 2
    share, width = out_grad.shape
    quarter = width // 4
    cut = quarter // 4
    shard = down_weight.shape[0]

    packed = call(
        pack_kernel, [shape(share, 2 * quarter)] * 2 + [shape(2 * shard, columns)] * 4, place, out_grad, down_weight
    )
    o_own, o_other, parts = packed[0], packed[1], packed[2:]

    parts = [parts[0]] + [send(parts[4 - k], z=4 - k) for k in (1, 2, 3)]
    block = pl.BlockSpec((share, columns), lambda n, place: (slot(place, n // 2, n % 2), 0))
    there = pl.BlockSpec((share, columns), lambda n, place: (n, 0))
    hid_own, *factors = call(
        hidden_kernel, [shape(tokens, columns)] * 3, place, *tied((gate_pre, up_pre), o_own),
        specs=[block] * 2, grid=(8,), to=[there] * 3,
    )
    o_l, o_h, o_lh = send(tied(o_other, hid_own), l=1), send(o_own, h=1), send(o_other, l=1, h=1)
    near, give_h = call(weight_kernel, [shape(4 * shard, columns)] * 2, place, *tied(parts, hid_own))
    near, far = [near], [send(give_h, h=1)]
    own, give = call(split_kernel, [shape(4 * share, quarter)] * 2, place, *tied((o_own, o_h, o_l, o_lh), hid_own, near[0]))
    near.append(ring_y(near[0]))
    hid_pair = send(tied(hid_own, near[1], o_h, o_l, o_lh), l=1)
    own, core = [own], [send(give, c=1)]
    own.append(ring_z(own[0]))
    core.append(ring_z(core[0]))
    far.append(ring_y(far[0]))
    near.append(ring_y(near[1]))
    own.append(ring_z(own[1]))
    core.append(ring_z(core[1]))
    far.append(ring_y(far[1]))
    near.append(ring_y(near[2]))
    own.append(ring_z(own[2]))
    core.append(ring_z(core[2]))
    far.append(ring_y(far[2]))
    weights = near + far
    hid_core = [send(tied(hid_own[: 2 * share], far[3], near[3], own[3]), c=1), send(tied(hid_own[2 * share :], far[3]), c=1)]

    (weight,) = call(rows_kernel, [shape(quarter, columns)], place, *weights)

    def hidden_grad(l, c, outs, *after, more=()):
        def kernel(*refs):
            product_kernel(l, len(outs), *refs)

        return call(
            kernel, outs, place, *tied((own, core)[c], *after), weight, *more,
            us=0.0 if l else 3.2, scratch=[pltpu.VMEM((tokens, quarter), BF16)],
        )

    factor = 1.0 / float(np.sqrt(np.float32(tokens * 16)))

    def term(s, *after):
        def kernel(*refs):
            term_kernel(s, factor, *refs)

        return call(
            kernel, [shape(cut, half)] * 2, place, *tied(own + core, *after), hid_own, *hid_core, hid_pair, hid_last,
            us=3.1, scratch=[pltpu.VMEM((4 * tokens, cut), BF16)],
        )

    out = [shape(tokens, half)] * 2
    (chip_out,) = hidden_grad(1, 1, [shape(tokens, columns)], hid_core[0])
    (mine,) = hidden_grad(1, 0, [shape(tokens, columns, dtype=F32)], chip_out)
    chip_out = send(chip_out, c=1)
    hid_last = send(tied(hid_pair, mine, hid_core[0]), c=1)
    sizes = [8]
    pairs = call(chip_kernel, [shape(n * share, columns) for n in sizes], place, mine, chip_out)
    first = term(1, pairs[0])
    second = term(2, first[0])
    core_out = [send(x, c=1) for x in hidden_grad(0, 1, out, second[0])]
    first = [ring_y(x) for x in first]
    second = [ring_y(added(a, b)) for a, b in zip(second, first)]
    third = term(3, first[0])
    third_0 = third[0]
    (mine,) = hidden_grad(0, 0, [shape(tokens, columns, dtype=F32)], third[0], second[0], more=core_out)
    third = [ring_y(added(a, b)) for a, b in zip(third, second)]
    pairs = [send(x, l=1) for x in pairs]
    last = term(0, third_0)
    (down_grad,) = call(join_kernel, [shape(cut, columns)], place, *last, *third)

    def gradients(first, pair, mine, *before):
        def kernel(*refs):
            gradient_kernel(first, *refs)

        count = pair.shape[0] // share
        hbm = pl.BlockSpec(memory_space=pltpu.HBM)
        return call(
            kernel, [shape(tokens, columns)] * 2, place, *factors, mine, pair, *before,
            specs=[VMEM] * 4 + [hbm] * len(before), to=[hbm] * 2, alias={5 + i: i for i in range(len(before))},
            scratch=[pltpu.VMEM((count, 2, share, columns), BF16), pltpu.SemaphoreType.DMA((count, 2))],
        )

    gate_grad, up_grad = gradients(0, pairs[0], tied(mine, down_grad))
    return (gate_grad, up_grad, down_grad)


def solution(mesh):
    return jax.shard_map(
        on_device,
        mesh=mesh,
        in_specs=(
            P("dp", "tensor"),
            P("dp", "tensor"),
            P(("dp", "tensor"), None),
            P(("dp", "tensor"), None),
        ),
        out_specs=(P("dp", "tensor"), P("dp", "tensor"), P("dp", "tensor")),
        check_vma=False,
    )
```

```python
import jax
import jax.numpy as jnp
import numpy as np
from jax import lax
from jax.experimental import pallas as pl
from jax.experimental.pallas import tpu as pltpu
from jax.sharding import PartitionSpec as P

SIZES = (4, 2, 2, 4, 2)
BF16, F32 = jnp.bfloat16, jnp.float32
VMEM = pl.BlockSpec(memory_space=pltpu.VMEM)
SMEM = pl.BlockSpec(memory_space=pltpu.SMEM)
EIGHT = [(k, j) for k in range(4) for j in range(2)]


def permuted(x, step):
    pairs = []
    for source in range(int(np.prod(SIZES))):
        place = [int(p) for p in np.unravel_index(source, SIZES)]
        target = [(p + d) % n for p, d, n in zip(place, step(place[2]), SIZES)]
        pairs.append((source, int(np.ravel_multi_index(target, SIZES))))
    return lax.ppermute(x, ("dp", "tensor"), pairs)


def send(x, y=0, l=0, c=0, z=0, h=0):
    return permuted(x, lambda core: (y, l, c, z, h))


def ring_y(x):
    return permuted(x, lambda core: (1 - 2 * core, 0, 0, 0, 0))


def ring_z(x):
    return permuted(x, lambda core: (0, 0, 0, 1 - 2 * core, 0))


def call(kernel, outs, place, *args, mib=24, specs=None, grid=None, to=None, scratch=(), us=0.0, alias=None):
    specs, to = specs or [VMEM] * len(args), to or [VMEM] * len(outs)
    if grid is None:
        placed = dict(in_specs=[SMEM] + specs, out_specs=to, scratch_shapes=scratch)
    else:
        placed = dict(
            grid_spec=pltpu.PrefetchScalarGridSpec(
                num_scalar_prefetch=1, grid=grid, in_specs=specs, out_specs=to, scratch_shapes=scratch
            )
        )
    return pl.pallas_call(
        kernel,
        out_shape=outs,
        input_output_aliases=alias or {},
        compiler_params=pltpu.CompilerParams(vmem_limit_bytes=mib << 20),
        cost_estimate=pl.CostEstimate(flops=int(us * 1.1e9), bytes_accessed=0, transcendentals=0),
        **placed,
    )(place, *args)


def shape(*dims, dtype=BF16):
    return jax.ShapeDtypeStruct(dims, dtype)


def at(start, size, step=128):
    return pl.ds(pl.multiple_of(start, step), size)


def slot(place, k, j):
    return (place[3] + k) % 4 * 2 + (place[4] + j) % 2


def behind(place, axis, s):
    return (place[axis] + 4 + (2 * place[2] - 1) * s) % 4


def chunk_rows(place, s, rows):
    return at((4 + (2 * place[2] - 1) * s) % 4 * rows, rows, 128)


def grad_kernel(place, grad, own, other):
    l, c = place[1], place[2]
    stripe = own.shape[1] // 8
    for out, side in ((own, l), (other, 1 - l)):
        for i, core in enumerate((c, 1 - c)):
            for k in range(4):
                to = pl.ds((i * 4 + k) * stripe, stripe)
                out[:, to] = grad[:, at((k * 4 + side * 2 + core) * stripe, stripe)]


def pack_kernel(place, weight, *parts):
    rows, columns = weight.shape[0], parts[0].shape[1]
    for n, (k, j) in enumerate(EIGHT):
        parts[k][j * rows : (j + 1) * rows, :] = weight[:, at(slot(place, k, j) * columns, columns)]


def split_kernel(place, *refs):
    parts, (keep, give) = refs[:4], refs[4:]
    rows, quarter = parts[0].shape[0], keep.shape[1]
    for n, part in enumerate(parts):
        keep[n * rows : (n + 1) * rows, :] = part[:, :quarter]
        give[n * rows : (n + 1) * rows, :] = part[:, quarter:]


def weight_kernel(place, *refs):
    parts, outs = refs[:4], refs[4:]
    rows = outs[0].shape[0] // 4
    for k, part in enumerate(parts):
        to = at((place[3] + k) % 4 * rows, rows, 32)
        for j, out in enumerate(outs):
            out[to, :] = part[j * rows : (j + 1) * rows, :]


def hidden_kernel(place, gate_ref, up_ref, out, gate_factor, up_factor):
    gate, up = gate_ref[...].astype(F32), up_ref[...].astype(F32)
    sig = jax.nn.sigmoid(gate)
    out[...] = (gate * sig * up).astype(BF16)
    gate_factor[...] = (up * sig * (1.0 + gate * (1.0 - sig))).astype(BF16)
    up_factor[...] = (gate * sig).astype(BF16)


def rows_kernel(place, *refs):
    weights, out = refs[:8], refs[8]
    cut = weights[0].shape[0] // 4
    for s in range(4):
        for j in range(2):
            for z in range(4):
                to = ((behind(place, 0, s) * 4 + z) * 2 + (place[4] + j) % 2) * cut
                out[at(to, cut, 32), :] = weights[4 * j + s][z * cut : (z + 1) * cut, :]


def product_kernel(l, count, place, *refs):
    chunks, weight, more, outs, rows_of = refs[:4], refs[4], refs[5 : -1 - count], refs[-1 - count : -1], refs[-1]
    rows = chunks[0].shape[0] // 2
    for s in range(4):
        rows_of[chunk_rows(place, s, rows), :] = chunks[s][l * rows : (l + 1) * rows, :]
    half = weight.shape[1] // 2
    for i in range(2):
        part = slice(i * half, (i + 1) * half)
        product = jnp.dot(rows_of[...], weight[:, part], preferred_element_type=F32)
        if more:
            product = product + more[i][...].astype(F32)
        if count == 1:
            outs[0][:, part] = product.astype(outs[0].dtype)
        else:
            outs[i][...] = product.astype(outs[i].dtype)


def term_kernel(s, factor, place, *refs):
    chunks, rights, outs, lhs = refs[:8], refs[8:13], refs[13:15], refs[15]
    rows = chunks[0].shape[0] // 2
    cut, half = outs[0].shape
    block = at(behind(place, 0, s) * cut, cut, 256)
    for n, chunk in enumerate(chunks):
        to = chunk_rows(place, n % 4, rows)
        for l in range(2):
            lhs.at[pl.ds((2 * l + n // 4) * 4 * rows, 4 * rows), :][to, :] = chunk[l * rows : (l + 1) * rows, block]
    for i, out in enumerate(outs):
        product, start = None, 0
        for right in rights:
            left = lhs[start : start + right.shape[0], :]
            part = lax.dot_general(
                left, right[:, i * half : (i + 1) * half], (((0,), (0,)), ((), ())), preferred_element_type=F32
            )
            product, start = part if product is None else product + part, start + right.shape[0]
        out[...] = (product * factor).astype(BF16)


def chip_kernel(place, mine, core, *outs):
    start = 0
    for out in outs:
        rows = slice(start, start + out.shape[0])
        out[...] = (mine[rows, :] + core[rows, :].astype(F32)).astype(BF16)
        start = rows.stop


def gradient_kernel(first, place, gate_factor, up_factor, mine, pair, *refs):
    outs, (stored, sem) = refs[-4:-2], refs[-2:]
    rows = mine.shape[0] // 8
    stores = []
    for n in range(pair.shape[0] // rows):
        here = slice((first + n) * rows, (first + n + 1) * rows)
        grad = mine[here, :] + pair[n * rows : (n + 1) * rows, :].astype(F32)
        block = at(slot(place, *EIGHT[first + n]) * rows, rows, 64)
        for i, (out, factor) in enumerate(zip(outs, (gate_factor, up_factor))):
            stored[n, i] = (grad * factor[here, :].astype(F32)).astype(BF16)
            stores.append(pltpu.make_async_copy(stored.at[n, i], out.at[block, :], sem.at[n, i]))
            stores[-1].start()
    for store in stores:
        store.wait()


def join_kernel(place, *refs):
    half = refs[0].shape[1]
    for i in range(2):
        total = refs[i][...].astype(F32) + refs[2 + i][...].astype(F32)
        refs[4][:, i * half : (i + 1) * half] = total.astype(BF16)


def tied(x, *first):
    return lax.optimization_barrier((x, first))[0]


def added(a, b):
    return (a.astype(F32) + b.astype(F32)).astype(BF16)


def on_device(gate_pre, up_pre, out_grad, down_weight):
    dp, tensor = lax.axis_index("dp"), lax.axis_index("tensor")
    place = jnp.stack([dp // 4, dp // 2 % 2, dp % 2, tensor // 2, tensor % 2]).astype(jnp.int32)
    tokens, columns = gate_pre.shape
    half = columns // 2
    share, width = out_grad.shape
    quarter = width // 4
    cut = quarter // 4
    shard = down_weight.shape[0]

    parts = call(pack_kernel, [shape(2 * shard, columns)] * 4, place, down_weight)
    o_own, o_other = call(grad_kernel, [shape(share, 2 * quarter)] * 2, place, tied(out_grad, parts[0]))

    parts = [parts[0]] + [send(parts[4 - k], z=4 - k) for k in (1, 2, 3)]
    block = pl.BlockSpec((share, columns), lambda n, place: (slot(place, n // 2, n % 2), 0))
    there = pl.BlockSpec((share, columns), lambda n, place: (n, 0))
    hid_own, *factors = call(
        hidden_kernel, [shape(tokens, columns)] * 3, place, *tied((gate_pre, up_pre), o_own),
        specs=[block] * 2, grid=(8,), to=[there] * 3,
    )
    o_l, o_h, o_lh = send(tied(o_other, hid_own), l=1), send(o_own, h=1), send(o_other, l=1, h=1)
    near, give_h = call(weight_kernel, [shape(4 * shard, columns)] * 2, place, *tied(parts, hid_own))
    near, far = [near], [send(give_h, h=1)]
    own, give = call(split_kernel, [shape(4 * share, quarter)] * 2, place, *tied((o_own, o_h, o_l, o_lh), hid_own, near[0]))
    near.append(ring_y(near[0]))
    hid_pair = send(tied(hid_own, near[1], o_h, o_l, o_lh), l=1)
    own, core = [own], [send(give, c=1)]
    own.append(ring_z(own[0]))
    core.append(ring_z(core[0]))
    far.append(ring_y(far[0]))
    near.append(ring_y(near[1]))
    own.append(ring_z(own[1]))
    core.append(ring_z(core[1]))
    far.append(ring_y(far[1]))
    near.append(ring_y(near[2]))
    own.append(ring_z(own[2]))
    core.append(ring_z(core[2]))
    far.append(ring_y(far[2]))
    weights = near + far
    hid_core = [send(tied(hid_own[: 2 * share], far[3], near[3], own[3]), c=1), send(tied(hid_own[2 * share :], far[3]), c=1)]

    (weight,) = call(rows_kernel, [shape(quarter, columns)], place, *weights)

    def hidden_grad(l, c, outs, *after, more=()):
        def kernel(*refs):
            product_kernel(l, len(outs), *refs)

        return call(
            kernel, outs, place, *tied((own, core)[c], *after), weight, *more,
            us=0.0 if l else 3.2, scratch=[pltpu.VMEM((tokens, quarter), BF16)],
        )

    factor = 1.0 / float(np.sqrt(np.float32(tokens * 16)))

    def term(s, *after):
        def kernel(*refs):
            term_kernel(s, factor, *refs)

        return call(
            kernel, [shape(cut, half)] * 2, place, *tied(own + core, *after), hid_own, *hid_core, hid_pair, hid_last,
            us=3.1, scratch=[pltpu.VMEM((4 * tokens, cut), BF16)],
        )

    out = [shape(tokens, half)] * 2
    (chip_out,) = hidden_grad(1, 1, [shape(tokens, columns)], hid_core[0])
    (mine,) = hidden_grad(1, 0, [shape(tokens, columns, dtype=F32)], chip_out)
    chip_out = send(chip_out, c=1)
    hid_last = send(tied(hid_pair, mine, hid_core[0]), c=1)
    sizes = [8]
    pairs = call(chip_kernel, [shape(n * share, columns) for n in sizes], place, mine, chip_out)
    first = term(1, pairs[0])
    second = term(2, first[0])
    core_out = [send(x, c=1) for x in hidden_grad(0, 1, out, second[0])]
    first = [ring_y(x) for x in first]
    second = [ring_y(added(a, b)) for a, b in zip(second, first)]
    third = term(3, first[0])
    third_0 = third[0]
    (mine,) = hidden_grad(0, 0, [shape(tokens, columns, dtype=F32)], third[0], second[0], more=core_out)
    third = [ring_y(added(a, b)) for a, b in zip(third, second)]
    pairs = [send(x, l=1) for x in pairs]
    last = term(0, third_0)
    (down_grad,) = call(join_kernel, [shape(cut, columns)], place, *last, *third)

    def gradients(first, pair, mine, *before):
        def kernel(*refs):
            gradient_kernel(first, *refs)

        count = pair.shape[0] // share
        hbm = pl.BlockSpec(memory_space=pltpu.HBM)
        return call(
            kernel, [shape(tokens, columns)] * 2, place, *factors, mine, pair, *before,
            specs=[VMEM] * 4 + [hbm] * len(before), to=[hbm] * 2, alias={5 + i: i for i in range(len(before))},
            scratch=[pltpu.VMEM((count, 2, share, columns), BF16), pltpu.SemaphoreType.DMA((count, 2))],
        )

    gate_grad, up_grad = gradients(0, pairs[0], tied(mine, down_grad))
    return (gate_grad, up_grad, down_grad)


def solution(mesh):
    return jax.shard_map(
        on_device,
        mesh=mesh,
        in_specs=(
            P("dp", "tensor"),
            P("dp", "tensor"),
            P(("dp", "tensor"), None),
            P(("dp", "tensor"), None),
        ),
        out_specs=(P("dp", "tensor"), P("dp", "tensor"), P("dp", "tensor")),
        check_vma=False,
    )
```
